256 devices in a mesh: ctx: 16 (over y, x_lo, core), head: 16 (over x_hi, z).
Axes of the slice: x: 4 (x_hi: 2, x_lo: 2; x = x_hi * 2 + x_lo), y: 4, z: 8, core: 2. Of those that a mesh axis runs over, the one named last changes fastest.
Arguments:
- inputs: bfloat16 [8192, 2048], P('ctx'), may hold values from -6 to 6
- tangents: bfloat16 [8192, 2048], P('ctx'), may hold values from -6 to 6
- w_qkv: bfloat16 [3, 2048, 2048], P(None, None, 'head'), may hold values from -0.125 to 0.125
- w_out: bfloat16 [2048, 2048], P('head'), may hold values from -0.1875 to 0.1875
Outputs:
- attended: bfloat16 [8192, 2048], P('ctx', 'head')
- attended_tangent: bfloat16 [8192, 2048], P('ctx', 'head')
The draws below stay inside these ranges and needn't reach their ends.
All inputs are finite; a program needn't handle non-finite values.
Results may differ from the reference program's by a relative error of at most 0.023.
Values may be sent and summed in bfloat16 or wider, within the bound.
A program may use at most 64 MiB of HBM per device.

```python
import math
import jax
import jax.numpy as jnp
from jax import lax

D = 2048
H = 16
HD = 128
TOKENS = 8192


def draw_inputs(key, part):
    key = jax.random.fold_in(key, 11)
    base_key = jax.random.fold_in(key, 0)
    base = jax.random.truncated_normal(base_key, -6.0, 6.0, (TOKENS, D), jnp.float32)
    return base.astype(jnp.bfloat16)


def with_spikes(array, stream_key, source, target, shards_of, factor):
    def block_of(dim):
        return (jnp.arange(array.shape[dim]) // (array.shape[dim] // shards_of)).reshape((-1,) + (1,) * (array.ndim - 1 - dim))

    one_side = jax.random.permutation(stream_key, shards_of)[block_of(target)]
    second = (block_of(target) + shards_of // 2) % shards_of
    return jnp.where((block_of(source) == one_side) | (block_of(source) == second), factor * array, array)


def block_scale(stream_key, dims, cuts, smallest, top_value):
    def one(position, shards_of):
        steps = jax.random.uniform(jax.random.fold_in(jax.random.fold_in(stream_key, 6), position), (shards_of,), jnp.float32, smallest / len(cuts), top_value / len(cuts))
        return jnp.repeat(jnp.exp(steps), dims[position] // shards_of).reshape((-1,) + (1,) * (len(dims) - position - 1))

    factor_of = one(*cuts[0])
    for cut in cuts[1:]:
        factor_of = factor_of * one(*cut)
    return factor_of


def gaussian(rng, shape, width, limit, cuts=(), kind=jnp.bfloat16):
    values = width * jax.random.normal(rng, shape, jnp.float32)
    if cuts:
        values = values * block_scale(rng, shape, cuts, -0.22, 0.18)
    return jnp.clip(values, -limit, limit).astype(kind)


def heavy_noise(stream_key, shape, deviation, bound, pieces, heavy, kind=jnp.bfloat16):
    drawn = deviation * jax.random.normal(stream_key, shape, jnp.float32)
    if pieces:
        drawn = drawn * block_scale(stream_key, shape, pieces, -0.22, 0.18)
    return jnp.clip(with_spikes(drawn, jax.random.fold_in(stream_key, 3), *heavy), -bound, bound).astype(kind)


def setup_inputs(seed: int = 0) -> dict:
    streams_of = jax.random.split(jax.random.key(seed), 5)
    return {
        "inputs": draw_inputs(jax.random.fold_in(streams_of[4], 71), 0),
        "tangents": gaussian(streams_of[1], (TOKENS, D), 1.0, 6.0, ((0, 16),)),
        "w_qkv": gaussian(streams_of[2], (3, D, H * HD), D ** -0.5, 0.125, ((2, 16),)),
        "w_out": heavy_noise(streams_of[3], (H * HD, D), (H * HD) ** -0.5, 0.1875, ((0, 16),), (0, 1, 16, 2.0)),
    }


def head_attention(packed):
    queries, keys, values, tqueries, tkeys, tvalues = packed
    block = math.gcd(TOKENS, 512)
    count = TOKENS // block
    scale = HD ** -0.5

    def one_block(item):
        qblock, tqblock = item
        scores = jnp.dot(qblock, keys.T, preferred_element_type=jnp.float32) * scale
        tscores = (jnp.dot(tqblock, keys.T, preferred_element_type=jnp.float32) + jnp.dot(qblock, tkeys.T, preferred_element_type=jnp.float32)) * scale
        top = jnp.max(scores, axis=1, keepdims=True)
        weights = jnp.exp(scores - top)
        total = jnp.sum(weights, axis=1, keepdims=True)
        spread = jnp.sum(weights * tscores, axis=1, keepdims=True)
        weights_b = weights.astype(jnp.bfloat16)
        mixed_b = (weights * tscores).astype(jnp.bfloat16)
        heads_out = jnp.dot(weights_b, values, preferred_element_type=jnp.float32) / total
        tangent_acc = jnp.dot(mixed_b, values, preferred_element_type=jnp.float32) + jnp.dot(weights_b, tvalues, preferred_element_type=jnp.float32)
        heads_tangent = tangent_acc / total - (spread / total) * heads_out
        return heads_out.astype(jnp.bfloat16), heads_tangent.astype(jnp.bfloat16)

    outs, touts = lax.map(one_block, (queries.reshape(count, block, HD), tqueries.reshape(count, block, HD)))
    return outs.reshape(TOKENS, HD), touts.reshape(TOKENS, HD)


def reference(inputs, tangents, w_qkv, w_out):
    def split(rows):
        return rows.reshape(TOKENS, H, HD).transpose(1, 0, 2)

    proj = [split(jnp.dot(inputs, w_qkv[j], preferred_element_type=jnp.float32).astype(jnp.bfloat16)) for j in range(3)]
    tproj = [split(jnp.dot(tangents, w_qkv[j], preferred_element_type=jnp.float32).astype(jnp.bfloat16)) for j in range(3)]
    outs, touts = lax.map(head_attention, (proj[0], proj[1], proj[2], tproj[0], tproj[1], tproj[2]))
    heads_out = outs.transpose(1, 0, 2).reshape(TOKENS, H * HD)
    heads_tangent = touts.transpose(1, 0, 2).reshape(TOKENS, H * HD)
    attended = jnp.dot(heads_out, w_out, preferred_element_type=jnp.float32).astype(jnp.bfloat16)
    attended_tangent = jnp.dot(heads_tangent, w_out, preferred_element_type=jnp.float32).astype(jnp.bfloat16)
    return attended, attended_tangent
```

```python
import functools
import math

import jax
import jax.numpy as jnp
from jax import lax
from jax.experimental import pallas as pl
from jax.experimental.pallas import tpu as pltpu
from jax.sharding import PartitionSpec as P

F32 = jnp.float32
BF16 = jnp.bfloat16
MESH = pl.DeviceIdType.MESH
HD = 128
D = 2048
TOK = 512
HALF = TOK // 2
NY, NX, NC = 4, 2, 2
NH, NZ = 2, 8
PIECE = TOK // NZ
LOG2E = math.log2(math.e)
LN2 = math.log(2.0)
SCALE = HD ** (-0.5)
ORDER = (4, 3, 5, 2, 6, 1, 7, 0)


def dot(a, b):
    return jnp.dot(a, b, preferred_element_type=F32)


def dot_nt(a, b):
    return lax.dot_general(a, b, (((1,), (1,)), ((), ())), preferred_element_type=F32)


def lane_sum(value):
    parts = [value[:, i : i + 128] for i in range(0, value.shape[1], 128)]
    return functools.reduce(lambda a, b: a + b, parts)


def kernel(
    x_hbm, t_hbm, wqkv_hbm, wout_hbm, out_ref, tout_ref,
    xt, wq, kv, qq, acc, top, total, spread,
    part_out, part_in, stat_out, stat_in, own_part, coef,
    a_out, a_in, w_all, f_out, f_in,
    ld, kv_s, kv_r, sib_s, sib_r, q_sem, w_s, w_r, ws_s, ws_r,
    p_s, p_r, st_sem, a_s, a_r, f_s, f_r,
):
    ctx = lax.axis_index("ctx")
    head = lax.axis_index("head")
    y, x, core = ctx // 4, (ctx // 2) % 2, ctx % 2
    xh, z = head // 8, head % 8

    def peer(dy=0, dx=0, dc=0, dh=0, dz=0):
        ny = lax.rem(y + (dy + NY), NY)
        nx = lax.rem(x + dx, NX)
        nc = lax.rem(core + dc, NC)
        nh = lax.rem(xh + dh, NH)
        nz = lax.rem(z + (dz + NZ), NZ)
        return ((ny * NX + nx) * NC + nc, nh * NZ + nz)

    def remote(src, dst, send, recv, device):
        return pltpu.make_async_remote_copy(
            src_ref=src, dst_ref=dst, send_sem=send, recv_sem=recv, device_id=device, device_id_type=MESH
        )

    friends = [peer(dc=1), peer(dx=1), peer(dy=1), peer(dy=-1)]
    friends += [peer(dh=b, dz=k) for b in range(NH) for k in range(NZ) if (b, k) != (0, 0)]
    barrier = pltpu.get_barrier_semaphore()
    for friend in friends:
        pl.semaphore_signal(barrier, inc=1, device_id=friend, device_id_type=MESH)

    def load(src, dst, index):
        copy = pltpu.make_async_copy(src, dst, ld.at[index])
        copy.start()
        return copy

    ld_k = load(wqkv_hbm.at[1], wq.at[:, 0:128], 0)
    ld_v = load(wqkv_hbm.at[2], wq.at[:, 128:256], 1)
    ld_x = [None, None]
    ld_t = [None, None]
    for h in range(2):
        rows = pl.ds(h * HALF, HALF)
        ld_x[h] = load(x_hbm.at[rows], xt.at[pl.ds(h * HALF, HALF)], 2 + h)
        ld_t[h] = load(t_hbm.at[rows], xt.at[pl.ds(TOK + h * HALF, HALF)], 4 + h)
    ld_q = load(wqkv_hbm.at[0], wq.at[:, 256:384], 6)
    ld_w = load(wout_hbm, w_all.at[0], 7)

    sends = []

    def start(copy):
        copy.start()
        sends.append(copy)
        return copy

    def project_kv(h):
        rows = pl.ds(h * 2 * HALF, HALF)
        ld_x[h].wait()
        both = dot(xt[pl.ds(h * HALF, HALF), :], wq[:, 0:256])
        kv[0, rows, 0:128] = both[:, 0:128].astype(BF16)
        kv[0, rows, 256:384] = both[:, 128:256].astype(BF16)
        ld_t[h].wait()
        both = dot(xt[pl.ds(TOK + h * HALF, HALF), :], wq[:, 0:256])
        kv[0, rows, 128:256] = (both[:, 0:128] * LN2).astype(BF16)
        kv[0, rows, 384:512] = both[:, 128:256].astype(BF16)

    def block(r, h):
        return kv.at[r, pl.ds(h * 2 * HALF, HALF)]

    def share(r, h):
        dst = kv.at[r, pl.ds(h * 2 * HALF + HALF, HALF)]
        return start(remote(block(r, h), dst, sib_s.at[r, h], sib_r.at[r, h], peer(dc=1)))

    def plus(r, h, index):
        to = (r + NY - 1) % NY
        return start(remote(block(r, h), block(to, h), kv_s.at[index], kv_r.at[to, h], peer(dy=1)))

    def minus(r, h, index):
        to = (r + 1) % NY
        return start(remote(block(r, h), block(to, h), kv_s.at[index], kv_r.at[to, h], peer(dy=-1)))

    def kv_arrived(r, h):
        remote(block(r, h), block(r, h), kv_s.at[0], kv_r.at[r, h], peer(dy=1)).wait_recv()

    def shared(r, h):
        dst = kv.at[r, pl.ds(h * 2 * HALF + HALF, HALF)]
        remote(dst, dst, sib_s.at[r, h], sib_r.at[r, h], peer(dc=1)).wait_recv()

    half_rows = pl.ds(pl.multiple_of(core * 64, 64), 64)

    def w_right(hop):
        rows = half_rows if hop < 3 else pl.ds(pl.multiple_of(core * 64, 64), 32)
        src, to = (NZ - hop) % NZ, NZ - 1 - hop
        start(remote(w_all.at[src, rows], w_all.at[to, rows], w_s.at[hop], w_r.at[to], peer(dz=1)))

    def w_left(hop):
        rows = half_rows if hop < 3 else pl.ds(pl.multiple_of(core * 64 + 32, 32), 32)
        src, to = hop, hop + 1
        sem = w_r.at[to] if hop < 3 else w_r.at[0]
        start(remote(w_all.at[src, rows], w_all.at[to, rows], w_s.at[4 + hop], sem, peer(dz=-1)))

    def w_arrived(slot):
        if slot == 4:
            rows = pl.ds(pl.multiple_of(core * 64, 64), 32)
            dst = w_all.at[4, rows]
            remote(dst, dst, w_s.at[0], w_r.at[4], peer(dz=1)).wait_recv()
            rows = pl.ds(pl.multiple_of(core * 64 + 32, 32), 32)
            dst = w_all.at[4, rows]
            remote(dst, dst, w_s.at[0], w_r.at[0], peer(dz=1)).wait_recv()
        else:
            dst = w_all.at[slot, half_rows]
            remote(dst, dst, w_s.at[0], w_r.at[slot], peer(dz=1)).wait_recv()
        src = w_all.at[slot, half_rows]
        start(remote(src, src, ws_s.at[slot], ws_r.at[slot], peer(dc=1)))

    def w_shared(slot):
        rows = pl.ds(pl.multiple_of((1 - core) * 64, 64), 64)
        dst = w_all.at[slot, rows]
        remote(dst, dst, ws_s.at[slot], ws_r.at[slot], peer(dc=1)).wait_recv()

    def w_hop(hop):
        w_arrived(NZ - hop)
        w_right(hop)
        w_arrived(hop)
        w_left(hop)

    def attend(lo, rows, r, key_lo, keys, first=False):
        rs = pl.ds(lo, rows)
        ks = pl.ds(key_lo, keys)
        scores = dot_nt(qq[rs, 128:256], kv[r, ks, 0:128])
        tscores = dot_nt(qq[rs, :], kv[r, ks, 0:256])
        peak = jnp.max(scores, axis=1, keepdims=True)
        if first:
            new_top = jnp.broadcast_to(peak, (rows, 128))
        else:
            old_top = top[rs, :]
            new_top = jnp.maximum(old_top, peak)
            factor = jnp.exp2(old_top - new_top)
        top[rs, :] = new_top
        weights = jnp.exp2(scores - new_top[:, 0:1])
        mixed = weights * tscores
        sum_w, sum_m = lane_sum(weights), lane_sum(mixed)
        add = dot(weights.astype(BF16), kv[r, ks, 256:512])
        add_m = dot(mixed.astype(BF16), kv[r, ks, 256:384])
        add_t = add[:, 128:256] + add_m
        if first:
            total[rs, :] = sum_w
            spread[rs, :] = sum_m
            acc[rs, 0:128] = add[:, 0:128]
            acc[rs, 128:256] = add_t
        else:
            total[rs, :] = total[rs, :] * factor + sum_w
            spread[rs, :] = spread[rs, :] * factor + sum_m
            acc[rs, 0:128] = acc[rs, 0:128] * factor + add[:, 0:128]
            acc[rs, 128:256] = acc[rs, 128:256] * factor + add_t

    def finish(lo):
        rs = pl.ds(lo, TOK)
        weight = jnp.sum(total[rs, :], axis=1, keepdims=True)
        inverse = 1.0 / weight
        mean = jnp.sum(spread[rs, :], axis=1, keepdims=True) * inverse
        out = acc[rs, 0:128] * inverse
        tangent = acc[rs, 128:256] * inverse - mean * out
        return out, tangent, top[rs, 0:1], weight, mean

    ld_k.wait()
    ld_v.wait()
    project_kv(0)
    pl.semaphore_wait(barrier, len(friends))
    plus(0, 0, 0)
    share(0, 0)
    project_kv(1)
    minus(0, 1, 3)
    plus(0, 1, 1)
    minus(0, 0, 4)
    share(0, 1)
    ld_w.wait()
    w_right(0)
    w_left(0)
    ld_q.wait()
    qq[TOK : 2 * TOK, 128:256] = (dot(xt[0:TOK, :], wq[:, 256:384]) * (SCALE * LOG2E)).astype(BF16)
    qq[TOK : 2 * TOK, 0:128] = (dot(xt[TOK : 2 * TOK, :], wq[:, 256:384]) * SCALE).astype(BF16)
    q_copy = start(remote(qq.at[pl.ds(TOK, TOK)], qq.at[pl.ds(0, TOK)], q_sem.at[0], q_sem.at[1], peer(dx=1)))

    shared(0, 0)
    shared(0, 1)
    attend(TOK, TOK, 0, 0, 1024, first=True)
    kv_arrived(3, 0)
    plus(3, 0, 2)
    share(3, 0)
    kv_arrived(1, 1)
    minus(1, 1, 5)
    share(1, 1)
    q_copy.wait_recv()
    attend(0, TOK, 0, 0, 1024, first=True)
    w_hop(1)
    shared(3, 0)
    attend(0, 2 * TOK, 3, 0, 512)
    shared(1, 1)
    attend(0, 2 * TOK, 1, 512, 512)
    kv_arrived(3, 1)
    share(3, 1)
    kv_arrived(1, 0)
    share(1, 0)
    w_hop(2)
    shared(3, 1)
    attend(0, 2 * TOK, 3, 512, 512)
    shared(1, 0)
    attend(0, 2 * TOK, 1, 0, 512)
    kv_arrived(2, 0)
    share(2, 0)
    kv_arrived(2, 1)
    share(2, 1)
    w_hop(3)
    shared(2, 0)
    attend(0, 2 * TOK, 2, 0, 512)
    shared(2, 1)
    attend(0, TOK, 2, 512, 512)

    out, tangent, peak, weight, mean = finish(0)
    part_out[:, 0:128] = out.astype(BF16)
    part_out[:, 128:256] = tangent.astype(BF16)
    lane = lax.broadcasted_iota(jnp.int32, (TOK, 128), 1)
    stats = jnp.where(lane == 0, peak, jnp.where(lane == 1, weight, mean))
    stat_out[...] = jnp.transpose(stats)[0:8, :]
    stat_copy = start(remote(stat_out, stat_in, st_sem.at[0], st_sem.at[1], peer(dx=1)))

    def piece(k):
        return pl.ds(pl.multiple_of(lax.rem(z + k, NZ) * PIECE, PIECE), PIECE)

    part_copies = {}
    for k in ORDER:
        rows = piece(k)
        part_copies[k] = start(remote(part_out.at[rows], part_in.at[rows], p_s.at[k], p_r.at[k], peer(dx=1)))
    attend(TOK, TOK, 2, 512, 512)
    out, tangent, peak, weight, mean = finish(TOK)
    own_part[:, 0:128] = out
    own_part[:, 128:256] = tangent
    stat_copy.wait_recv()
    padded = jnp.concatenate([stat_in[...], jnp.zeros((120, TOK), F32)], axis=0)
    other = jnp.transpose(padded)
    peak2, weight2, mean2 = other[:, 0:1], other[:, 1:2], other[:, 2:3]
    high = jnp.maximum(peak, peak2)
    mass = weight * jnp.exp2(peak - high)
    mass2 = weight2 * jnp.exp2(peak2 - high)
    inverse = 1.0 / (mass + mass2)
    p1, p2 = mass * inverse, mass2 * inverse
    coef[0] = jnp.broadcast_to(p1, (TOK, 128))
    coef[1] = jnp.broadcast_to(p2, (TOK, 128))
    coef[2] = jnp.broadcast_to(p1 * p2 * (mean - mean2), (TOK, 128))

    a_copies = {}
    for k in ORDER:
        rows = piece(k)
        part_copies[k].wait_recv()
        o1, u1 = own_part[rows, 0:128], own_part[rows, 128:256]
        o2, u2 = part_in[rows, 0:128].astype(F32), part_in[rows, 128:256].astype(F32)
        c1, c2, c3 = coef[0, rows, :], coef[1, rows, :], coef[2, rows, :]
        merged = (c1 * o1 + c2 * o2).astype(BF16)
        tmerged = (c1 * u1 + c2 * u2 + c3 * (o1 - o2)).astype(BF16)
        if k == 0:
            a_in[0:PIECE, 0:128] = merged
            a_in[PIECE : 2 * PIECE, 0:128] = tmerged
        else:
            a_out[k, 0:PIECE, :] = merged
            a_out[k, PIECE : 2 * PIECE, :] = tmerged
            back = NZ - k
            dst = a_in.at[:, back * 128 : back * 128 + 128]
            a_copies[k] = start(remote(a_out.at[k], dst, a_s.at[k], a_r.at[back], peer(dz=k)))

    w_arrived(4)
    for slot in range(1, NZ):
        w_shared(slot)
    for k in range(1, NZ):
        a_copies[k].wait_recv()

    f_copies = {}
    for k in ORDER:
        for b in (1, 0):
            column = (lax.rem(xh + b, NH) * NZ + lax.rem(z + k, NZ)) * 128
            rhs = w_all[:, :, pl.ds(pl.multiple_of(column, 128), 128)].reshape(NZ * 128, 128)
            term = dot(a_in[...], rhs).astype(BF16)
            if (b, k) == (0, 0):
                f_in[0, 0] = term
            else:
                f_out[b, k] = term
                back = (NZ - k) % NZ
                f_copies[b, k] = start(
                    remote(f_out.at[b, k], f_in.at[b, back], f_s.at[b, k], f_r.at[b, back], peer(dh=b, dz=k))
                )
    for k in range(NZ):
        for b in range(NH):
            if (b, k) != (0, 0):
                remote(f_out.at[b, k], f_in.at[b, k], f_s.at[b, k], f_r.at[b, k], peer(dh=b, dz=k)).wait_recv()
        rows = piece(k)
        summed = f_in[0, k].astype(F32) + f_in[1, k].astype(F32)
        out_ref[rows, :] = summed[0:PIECE].astype(BF16)
        tout_ref[rows, :] = summed[PIECE : 2 * PIECE].astype(BF16)
    for copy in sends:
        copy.wait_send()


def local(inputs, tangents, w_qkv, w_out):
    dma = pltpu.SemaphoreType.DMA
    vmem = pltpu.VMEM
    return pl.pallas_call(
        kernel,
        name="tangent_attention",
        out_shape=[jax.ShapeDtypeStruct((TOK, 128), BF16)] * 2,
        in_specs=[pl.BlockSpec(memory_space=pl.ANY)] * 4,
        out_specs=[pl.BlockSpec(memory_space=pltpu.VMEM)] * 2,
        scratch_shapes=[
            vmem((2 * TOK, D), BF16),
            vmem((D, 384), BF16),
            vmem((NY, 1024, 512), BF16),
            vmem((2 * TOK, 256), BF16),
            vmem((2 * TOK, 256), F32),
            vmem((2 * TOK, 128), F32),
            vmem((2 * TOK, 128), F32),
            vmem((2 * TOK, 128), F32),
            vmem((TOK, 256), BF16),
            vmem((TOK, 256), BF16),
            vmem((8, TOK), F32),
            vmem((8, TOK), F32),
            vmem((TOK, 256), F32),
            vmem((3, TOK, 128), F32),
            vmem((NZ, 128, 128), BF16),
            vmem((128, NZ * 128), BF16),
            vmem((NZ, 128, D), BF16),
            vmem((NH, NZ, 128, 128), BF16),
            vmem((NH, NZ, 128, 128), BF16),
            dma((8,)),
            dma((6,)),
            dma((NY, 2)),
            dma((NY, 2)),
            dma((NY, 2)),
            dma((2,)),
            dma((8,)),
            dma((8,)),
            dma((8,)),
            dma((8,)),
            dma((8,)),
            dma((8,)),
            dma((2,)),
            dma((8,)),
            dma((8,)),
            dma((NH, NZ)),
            dma((NH, NZ)),
        ],
        compiler_params=pltpu.CompilerParams(
            collective_id=0, has_side_effects=True, vmem_limit_bytes=58 * 2**20
        ),
    )(inputs, tangents, w_qkv, w_out)


def solution(mesh):
    return jax.shard_map(
        local,
        mesh=mesh,
        in_specs=(P("ctx", None), P("ctx", None), P(None, None, "head"), P("head", None)),
        out_specs=(P("ctx", "head"), P("ctx", "head")),
        check_vma=False,
    )
```

```python
import functools
import math

import jax
import jax.numpy as jnp
from jax import lax
from jax.experimental import pallas as pl
from jax.experimental.pallas import tpu as pltpu
from jax.sharding import PartitionSpec as P

F32 = jnp.float32
BF16 = jnp.bfloat16
MESH = pl.DeviceIdType.MESH
HD = 128
D = 2048
TOK = 512
HALF = TOK // 2
NY, NX, NC = 4, 2, 2
NH, NZ = 2, 8
PIECE = TOK // NZ
LOG2E = math.log2(math.e)
LN2 = math.log(2.0)
SCALE = HD ** (-0.5)
ORDER = (4, 3, 5, 2, 6, 1, 7, 0)


def dot(a, b):
    return jnp.dot(a, b, preferred_element_type=F32)


def dot_nt(a, b):
    return lax.dot_general(a, b, (((1,), (1,)), ((), ())), preferred_element_type=F32)


def lane_sum(value):
    parts = [value[:, i : i + 128] for i in range(0, value.shape[1], 128)]
    return functools.reduce(lambda a, b: a + b, parts)


def kernel(
    x_hbm, t_hbm, wqkv_hbm, wout_hbm, result,
    xt, wq, kv, qq, acc, top, total, spread,
    part_out, part_in, stat_out, stat_in, own_part, coef,
    a_out, a_in, w_all, g_out, g_in, g_own, f_out,
    ld, kv_s, kv_r, sib_s, sib_r, q_sem, w_s, w_r, ws_s, ws_r,
    p_s, p_r, st_sem, a_s, a_r, g_s, g_r, f_s, f_r,
):
    ctx = lax.axis_index("ctx")
    head = lax.axis_index("head")
    y, x, core = ctx // 4, (ctx // 2) % 2, ctx % 2
    xh, z = head // 8, head % 8

    def peer(dy=0, dx=0, dc=0, dh=0, dz=0):
        ny = lax.rem(y + (dy + NY), NY)
        nx = lax.rem(x + dx, NX)
        nc = lax.rem(core + dc, NC)
        nh = lax.rem(xh + dh, NH)
        nz = lax.rem(z + (dz + NZ), NZ)
        return ((ny * NX + nx) * NC + nc, nh * NZ + nz)

    def remote(src, dst, send, recv, device):
        return pltpu.make_async_remote_copy(
            src_ref=src, dst_ref=dst, send_sem=send, recv_sem=recv, device_id=device, device_id_type=MESH
        )

    friends = [peer(dc=1), peer(dx=1), peer(dy=1), peer(dy=-1)]
    friends += [peer(dz=k) for k in range(1, NZ)] + [peer(dh=1)]
    barrier = pltpu.get_barrier_semaphore()
    for friend in friends:
        pl.semaphore_signal(barrier, inc=1, device_id=friend, device_id_type=MESH)

    def load(src, dst, index):
        copy = pltpu.make_async_copy(src, dst, ld.at[index])
        copy.start()
        return copy

    ld_k = load(wqkv_hbm.at[1], wq.at[:, 0:128], 0)
    ld_v = load(wqkv_hbm.at[2], wq.at[:, 128:256], 1)
    ld_x = [None, None]
    ld_t = [None, None]
    for h in range(2):
        rows = pl.ds(h * HALF, HALF)
        ld_x[h] = load(x_hbm.at[rows], xt.at[pl.ds(2 * h * HALF, HALF)], 2 + h)
        ld_t[h] = load(t_hbm.at[rows], xt.at[pl.ds(2 * h * HALF + HALF, HALF)], 4 + h)
    ld_w = load(wout_hbm, w_all.at[0], 7)
    ld_q = load(wqkv_hbm.at[0], wq.at[:, 256:384], 6)

    def start(copy):
        copy.start()
        return copy

    def sent(sem, src):
        remote(src, src, sem, q_sem.at[1], peer(dc=1)).wait_send()

    def project_kv(h):
        rows = pl.ds(h * 2 * HALF, HALF)
        ld_x[h].wait()
        ld_t[h].wait()
        flat = dot(xt[pl.ds(h * 2 * HALF, HALF), :], wq[:, 0:256])
        tflat = dot(xt[pl.ds(h * 2 * HALF + HALF, HALF), :], wq[:, 0:256])
        kv[0, rows, 0:128] = flat[:, 0:128].astype(BF16)
        kv[0, rows, 256:384] = flat[:, 128:256].astype(BF16)
        kv[0, rows, 128:256] = (tflat[:, 0:128] * LN2).astype(BF16)
        kv[0, rows, 384:512] = tflat[:, 128:256].astype(BF16)

    def block(r, h):
        return kv.at[r, pl.ds(h * HALF if r == 2 else h * 2 * HALF, HALF)]

    def other(r, h):
        return kv.at[r, pl.ds(h * HALF + 2 * HALF if r == 2 else h * 2 * HALF + HALF, HALF)]

    def share(r, h):
        dst = other(r, h)
        return start(remote(block(r, h), dst, sib_s.at[0], sib_r.at[r, h], peer(dc=1)))

    def plus(r, h):
        to = (r + NY - 1) % NY
        return start(remote(block(r, h), block(to, h), kv_s.at[0], kv_r.at[to, h], peer(dy=1)))

    def minus(r, h):
        to = (r + 1) % NY
        return start(remote(block(r, h), block(to, h), kv_s.at[0], kv_r.at[to, h], peer(dy=-1)))

    def kv_arrived(r, h):
        remote(block(r, h), block(r, h), kv_s.at[0], kv_r.at[r, h], peer(dy=1)).wait_recv()

    def shared(r, h):
        dst = other(r, h)
        remote(dst, dst, sib_s.at[0], sib_r.at[r, h], peer(dc=1)).wait_recv()

    half_rows = pl.ds(pl.multiple_of(core * 64, 64), 64)

    def w_right(hop):
        rows = half_rows if hop < 3 else pl.ds(pl.multiple_of(core * 64, 64), 32)
        src, to = (NZ - hop) % NZ, NZ - 1 - hop
        start(remote(w_all.at[src, rows], w_all.at[to, rows], w_s.at[0], w_r.at[to], peer(dz=1)))

    def w_left(hop):
        rows = half_rows if hop < 3 else pl.ds(pl.multiple_of(core * 64 + 32, 32), 32)
        src, to = hop, hop + 1
        sem = w_r.at[to] if hop < 3 else w_r.at[0]
        start(remote(w_all.at[src, rows], w_all.at[to, rows], w_s.at[0], sem, peer(dz=-1)))

    def w_arrived(slot):
        if slot == 4:
            rows = pl.ds(pl.multiple_of(core * 64, 64), 32)
            dst = w_all.at[4, rows]
            remote(dst, dst, w_s.at[0], w_r.at[4], peer(dz=1)).wait_recv()
            rows = pl.ds(pl.multiple_of(core * 64 + 32, 32), 32)
            dst = w_all.at[4, rows]
            remote(dst, dst, w_s.at[0], w_r.at[0], peer(dz=1)).wait_recv()
        else:
            dst = w_all.at[slot, half_rows]
            remote(dst, dst, w_s.at[0], w_r.at[slot], peer(dz=1)).wait_recv()
        src = w_all.at[slot, half_rows]
        start(remote(src, src, ws_s.at[0], ws_r.at[slot], peer(dc=1)))

    def w_shared(slot):
        rows = pl.ds(pl.multiple_of((1 - core) * 64, 64), 64)
        dst = w_all.at[slot, rows]
        remote(dst, dst, ws_s.at[0], ws_r.at[slot], peer(dc=1)).wait_recv()

    def w_hop(hop):
        w_arrived(NZ - hop)
        w_right(hop)
        w_arrived(hop)
        w_left(hop)

    def attend(lo, rows, r, key_lo, keys, first=False):
        rs = pl.ds(lo, rows)
        ks = pl.ds(key_lo, keys)
        scores = dot_nt(qq[rs, 128:256], kv[r, ks, 0:128])
        tscores = dot_nt(qq[rs, :], kv[r, ks, 0:256])
        peak = jnp.max(scores, axis=1, keepdims=True)
        if first:
            new_top = jnp.broadcast_to(peak, (rows, 128))
        else:
            old_top = top[rs, :]
            new_top = jnp.maximum(old_top, peak)
            factor = jnp.exp2(old_top - new_top)
        top[rs, :] = new_top
        weights = jnp.exp2(scores - new_top[:, 0:1])
        mixed = weights * tscores
        sum_w, sum_m = lane_sum(weights), lane_sum(mixed)
        weights, mixed = weights.astype(BF16), mixed.astype(BF16)
        if first:
            total[rs, :] = sum_w
            spread[rs, :] = sum_m
        else:
            total[rs, :] = total[rs, :] * factor + sum_w
            spread[rs, :] = spread[rs, :] * factor + sum_m
        step = rows // 2
        for i in (0, step):
            add = dot(weights[i : i + step], kv[r, ks, 256:512])
            add_m = dot(mixed[i : i + step], kv[r, ks, 256:384])
            add_t = add[:, 128:256] + add_m
            ps = pl.ds(lo + i, step)
            if first:
                acc[ps, 0:128] = add[:, 0:128]
                acc[ps, 128:256] = add_t
            else:
                part = factor[i : i + step]
                acc[ps, 0:128] = acc[ps, 0:128] * part + add[:, 0:128]
                acc[ps, 128:256] = acc[ps, 128:256] * part + add_t

    def finish(lo):
        rs = pl.ds(lo, TOK)
        weight = jnp.sum(total[rs, :], axis=1, keepdims=True)
        inverse = 1.0 / weight
        mean = jnp.sum(spread[rs, :], axis=1, keepdims=True) * inverse
        out = acc[rs, 0:128] * inverse
        tangent = acc[rs, 128:256] * inverse - mean * out
        return out, tangent, top[rs, 0:1], weight, mean

    ld_k.wait()
    ld_v.wait()
    project_kv(0)
    ld_w.wait()
    pl.semaphore_wait(barrier, len(friends))
    plus(0, 0)
    w_right(0)
    w_left(0)
    share(0, 0)
    project_kv(1)
    minus(0, 1)
    plus(0, 1)
    minus(0, 0)
    share(0, 1)
    ld_q.wait()
    for h in range(2):
        rows = pl.ds(TOK + h * HALF, HALF)
        flat = dot(xt[pl.ds(h * 2 * HALF, HALF), :], wq[:, 256:384])
        tflat = dot(xt[pl.ds(h * 2 * HALF + HALF, HALF), :], wq[:, 256:384])
        qq[rows, 128:256] = (flat * (SCALE * LOG2E)).astype(BF16)
        qq[rows, 0:128] = (tflat * SCALE).astype(BF16)
    q_copy = start(remote(qq.at[pl.ds(TOK, TOK)], qq.at[pl.ds(0, TOK)], q_sem.at[0], q_sem.at[1], peer(dx=1)))

    shared(0, 0)
    shared(0, 1)
    attend(TOK, TOK, 0, 0, 1024, first=True)
    kv_arrived(3, 0)
    plus(3, 0)
    share(3, 0)
    kv_arrived(1, 1)
    minus(1, 1)
    share(1, 1)
    w_hop(1)
    q_copy.wait_recv()
    attend(0, TOK, 0, 0, 1024, first=True)
    shared(3, 0)
    attend(0, 2 * TOK, 3, 0, 512)
    kv_arrived(3, 1)
    share(3, 1)
    kv_arrived(1, 0)
    share(1, 0)
    shared(1, 1)
    attend(0, 2 * TOK, 1, 512, 512)
    w_hop(2)
    shared(3, 1)
    attend(0, 2 * TOK, 3, 512, 512)
    kv_arrived(2, 0)
    share(2, 0)
    kv_arrived(2, 1)
    share(2, 1)
    shared(1, 0)
    attend(0, 2 * TOK, 1, 0, 512)
    attend(0, 2 * TOK, 2, 0, 512)
    shared(2, 0)
    shared(2, 1)
    attend(0, TOK, 2, 512, 512)

    out, tangent, peak, weight, mean = finish(0)
    part_out[:, 0:128] = out.astype(BF16)
    part_out[:, 128:256] = tangent.astype(BF16)
    lane = lax.broadcasted_iota(jnp.int32, (TOK, 128), 1)
    stats = jnp.where(lane == 0, peak, jnp.where(lane == 1, weight, mean))
    stat_out[...] = jnp.transpose(stats)[0:8, :]
    stat_copy = start(remote(stat_out, stat_in, st_sem.at[0], st_sem.at[1], peer(dx=1)))

    def piece(k):
        return pl.ds(pl.multiple_of(lax.rem(z + k, NZ) * PIECE, PIECE), PIECE)

    part_copies = {}
    for k in ORDER:
        rows = piece(k)
        part_copies[k] = start(remote(part_out.at[rows], part_in.at[rows], p_s.at[0], p_r.at[k], peer(dx=1)))
    w_hop(3)
    attend(TOK, TOK, 2, 512, 512)
    out, tangent, peak, weight, mean = finish(TOK)
    own_part[:, 0:128] = out
    own_part[:, 128:256] = tangent
    stat_copy.wait_recv()
    padded = jnp.concatenate([stat_in[...], jnp.zeros((120, TOK), F32)], axis=0)
    other = jnp.transpose(padded)
    peak2, weight2, mean2 = other[:, 0:1], other[:, 1:2], other[:, 2:3]
    high = jnp.maximum(peak, peak2)
    mass = weight * jnp.exp2(peak - high)
    mass2 = weight2 * jnp.exp2(peak2 - high)
    inverse = 1.0 / (mass + mass2)
    p1, p2 = mass * inverse, mass2 * inverse
    coef[0] = jnp.broadcast_to(p1, (TOK, 128))
    coef[1] = jnp.broadcast_to(p2, (TOK, 128))
    coef[2] = jnp.broadcast_to(p1 * p2 * (mean - mean2), (TOK, 128))

    a_copies = {}
    for k in ORDER:
        rows = piece(k)
        part_copies[k].wait_recv()
        o1, u1 = own_part[rows, 0:128], own_part[rows, 128:256]
        o2, u2 = part_in[rows, 0:128].astype(F32), part_in[rows, 128:256].astype(F32)
        c1, c2, c3 = coef[0, rows, :], coef[1, rows, :], coef[2, rows, :]
        merged = (c1 * o1 + c2 * o2).astype(BF16)
        tmerged = (c1 * u1 + c2 * u2 + c3 * (o1 - o2)).astype(BF16)
        if k == 0:
            a_in[0:PIECE, 0:128] = merged
            a_in[PIECE : 2 * PIECE, 0:128] = tmerged
        else:
            a_out[k, 0:PIECE, :] = merged
            a_out[k, PIECE : 2 * PIECE, :] = tmerged
            back = NZ - k
            dst = a_in.at[:, back * 128 : back * 128 + 128]
            a_copies[k] = start(remote(a_out.at[k], dst, a_s.at[0], a_r.at[back], peer(dz=k)))

    w_arrived(4)
    for slot in range(1, NZ):
        w_shared(slot)
    for k in range(1, NZ):
        a_copies[k].wait_recv()

    def columns(b, k):
        column = (lax.rem(xh + b, NH) * NZ + lax.rem(z + k, NZ)) * 128
        return w_all[:, :, pl.ds(pl.multiple_of(column, 128), 128)].reshape(NZ * 128, 128)

    g_copies = {}
    for k in ORDER:
        both = dot(a_in[...], jnp.concatenate([columns(1, k), columns(0, k)], axis=1))
        g_out[k] = both[:, 0:128].astype(BF16)
        g_copies[k] = start(remote(g_out.at[k], g_in.at[k], g_s.at[0], g_r.at[k], peer(dh=1)))
        g_own[k] = both[:, 128:256]
    for k in ORDER:
        g_copies[k].wait_recv()
        f_out[k] = (g_own[k] + g_in[k].astype(F32)).astype(BF16)
        if k == 0:
            mine = pltpu.make_async_copy(f_out.at[0], result.at[z], f_r.at[0])
            mine.start()
        else:
            start(remote(f_out.at[k], result.at[z], f_s.at[0], f_r.at[NZ - k], peer(dz=k)))
    sent(kv_s.at[0], xt.at[pl.ds(0, 6 * 64)])
    sent(sib_s.at[0], xt.at[pl.ds(0, 8 * 64)])
    sent(w_s.at[0], xt.at[pl.ds(0, 7 * 64)])
    sent(ws_s.at[0], xt.at[pl.ds(0, 7 * 64)])
    sent(p_s.at[0], part_out)
    sent(a_s.at[0], a_out.at[pl.ds(1, NZ - 1)])
    sent(g_s.at[0], g_out)
    q_copy.wait_send()
    stat_copy.wait_send()
    mine.wait()
    for k in range(1, NZ):
        dst = result.at[lax.rem(z + k, NZ)]
        remote(f_out.at[k], dst, f_s.at[0], f_r.at[k], peer(dz=k)).wait_recv()
    sent(f_s.at[0], f_out.at[pl.ds(1, NZ - 1)])


def split(result, out, tout):
    out[...] = result[:, 0:PIECE, :]
    tout[...] = result[:, PIECE : 2 * PIECE, :]


def local(inputs, tangents, w_qkv, w_out):
    dma = pltpu.SemaphoreType.DMA
    vmem = pltpu.VMEM
    result = pl.pallas_call(
        kernel,
        name="tangent_attention",
        out_shape=jax.ShapeDtypeStruct((NZ, 2 * PIECE, 128), BF16),
        in_specs=[pl.BlockSpec(memory_space=pl.ANY)] * 4,
        out_specs=pl.BlockSpec(memory_space=pl.ANY),
        scratch_shapes=[
            vmem((2 * TOK, D), BF16),
            vmem((D, 384), BF16),
            vmem((NY, 1024, 512), BF16),
            vmem((2 * TOK, 256), BF16),
            vmem((2 * TOK, 256), F32),
            vmem((2 * TOK, 128), F32),
            vmem((2 * TOK, 128), F32),
            vmem((2 * TOK, 128), F32),
            vmem((TOK, 256), BF16),
            vmem((TOK, 256), BF16),
            vmem((8, TOK), F32),
            vmem((8, TOK), F32),
            vmem((TOK, 256), F32),
            vmem((3, TOK, 128), F32),
            vmem((NZ, 128, 128), BF16),
            vmem((128, NZ * 128), BF16),
            vmem((NZ, 128, D), BF16),
            vmem((NZ, 128, 128), BF16),
            vmem((NZ, 128, 128), BF16),
            vmem((NZ, 128, 128), F32),
            vmem((NZ, 128, 128), BF16),
            dma((8,)),
            dma((1,)),
            dma((NY, 2)),
            dma((1,)),
            dma((NY, 2)),
            dma((2,)),
            dma((1,)),
            dma((8,)),
            dma((1,)),
            dma((8,)),
            dma((1,)),
            dma((8,)),
            dma((2,)),
            dma((1,)),
            dma((8,)),
            dma((1,)),
            dma((8,)),
            dma((1,)),
            dma((8,)),
        ],
        compiler_params=pltpu.CompilerParams(
            collective_id=0, has_side_effects=True, vmem_limit_bytes=58 * 2**20
        ),
    )(inputs, tangents, w_qkv, w_out)
    out, tout = pl.pallas_call(
        split,
        name="split",
        out_shape=[jax.ShapeDtypeStruct((NZ, PIECE, 128), BF16)] * 2,
        in_specs=[pl.BlockSpec(memory_space=pltpu.VMEM)],
        out_specs=[pl.BlockSpec(memory_space=pltpu.VMEM)] * 2,
    )(result)
    return out.reshape(TOK, 128), tout.reshape(TOK, 128)


def solution(mesh):
    return jax.shard_map(
        local,
        mesh=mesh,
        in_specs=(P("ctx", None), P("ctx", None), P(None, None, "head"), P("head", None)),
        out_specs=(P("ctx", "head"), P("ctx", "head")),
        check_vma=False,
    )
```

```python
import functools
import math

import jax
import jax.numpy as jnp
from jax import lax
from jax.experimental import pallas as pl
from jax.experimental.pallas import tpu as pltpu
from jax.sharding import PartitionSpec as P

F32 = jnp.float32
BF16 = jnp.bfloat16
MESH = pl.DeviceIdType.MESH
HD = 128
D = 2048
TOK = 512
HALF = TOK // 2
NY, NX, NC = 4, 2, 2
NH, NZ = 2, 8
PIECE = TOK // NZ
LOG2E = math.log2(math.e)
LN2 = math.log(2.0)
SCALE = HD ** (-0.5)
ORDER = (4, 3, 5, 2, 6, 1, 7, 0)


def dot(a, b):
    return jnp.dot(a, b, preferred_element_type=F32)


def dot_nt(a, b):
    return lax.dot_general(a, b, (((1,), (1,)), ((), ())), preferred_element_type=F32)


def lane_sum(value):
    parts = [value[:, i : i + 128] for i in range(0, value.shape[1], 128)]
    return functools.reduce(lambda a, b: a + b, parts)


def kernel(
    x_hbm, t_hbm, wqkv_hbm, wout_hbm, both_ref,
    xt, wq, kv, qq, acc, top, total, spread,
    part_out, part_in, stat_out, stat_in, own_part, coef,
    a_out, a_in, w_all, g_out, g_in, g_own, f_out, f_in,
    ld, kv_s, kv_r, sib_s, sib_r, q_sem, w_s, w_r, ws_s, ws_r,
    p_s, p_r, st_sem, a_s, a_r, g_s, g_r, f_s, f_r,
):
    out_ref, tout_ref = both_ref.at[pl.ds(0, TOK)], both_ref.at[pl.ds(TOK, TOK)]
    ctx = lax.axis_index("ctx")
    head = lax.axis_index("head")
    y, x, core = ctx // 4, (ctx // 2) % 2, ctx % 2
    xh, z = head // 8, head % 8

    def peer(dy=0, dx=0, dc=0, dh=0, dz=0):
        ny = lax.rem(y + (dy + NY), NY)
        nx = lax.rem(x + dx, NX)
        nc = lax.rem(core + dc, NC)
        nh = lax.rem(xh + dh, NH)
        nz = lax.rem(z + (dz + NZ), NZ)
        return ((ny * NX + nx) * NC + nc, nh * NZ + nz)

    def remote(src, dst, send, recv, device):
        return pltpu.make_async_remote_copy(
            src_ref=src, dst_ref=dst, send_sem=send, recv_sem=recv, device_id=device, device_id_type=MESH
        )

    friends = [peer(dc=1), peer(dx=1), peer(dy=1), peer(dy=-1)]
    friends += [peer(dz=k) for k in range(1, NZ)] + [peer(dh=1)]
    barrier = pltpu.get_barrier_semaphore()
    for friend in friends:
        pl.semaphore_signal(barrier, inc=1, device_id=friend, device_id_type=MESH)

    def load(src, dst, index):
        copy = pltpu.make_async_copy(src, dst, ld.at[index])
        copy.start()
        return copy

    def load_rows(h):
        rows = pl.ds(h * HALF, HALF)
        first = load(x_hbm.at[rows], xt.at[pl.ds(2 * h * HALF, HALF)], 2 + h)
        return first, load(t_hbm.at[rows], xt.at[pl.ds(2 * h * HALF + HALF, HALF)], 4 + h)

    ld_k = load(wqkv_hbm.at[1], wq.at[:, 0:128], 0)
    ld_v = load(wqkv_hbm.at[2], wq.at[:, 128:256], 1)
    ld_rows = [load_rows(0)]

    def start(copy):
        copy.start()
        return copy

    def sent(sem, src):
        remote(src, src, sem, q_sem.at[1], peer(dc=1)).wait_send()

    def project_kv(h):
        rows = pl.ds(h * 2 * HALF, HALF)
        ld_rows[h][0].wait()
        ld_rows[h][1].wait()
        flat = dot(xt[pl.ds(h * 2 * HALF, HALF), :], wq[:, 0:256])
        tflat = dot(xt[pl.ds(h * 2 * HALF + HALF, HALF), :], wq[:, 0:256])
        kv[0, rows, 0:128] = flat[:, 0:128].astype(BF16)
        kv[0, rows, 256:384] = flat[:, 128:256].astype(BF16)
        kv[0, rows, 128:256] = (tflat[:, 0:128] * LN2).astype(BF16)
        kv[0, rows, 384:512] = tflat[:, 128:256].astype(BF16)

    def block(r, h):
        return kv.at[r, pl.ds(h * HALF if r == 2 else h * 2 * HALF, HALF)]

    def other(r, h):
        return kv.at[r, pl.ds(h * HALF + 2 * HALF if r == 2 else h * 2 * HALF + HALF, HALF)]

    def share(r, h):
        dst = other(r, h)
        return start(remote(block(r, h), dst, sib_s.at[0], sib_r.at[r, h], peer(dc=1)))

    def plus(r, h):
        to = (r + NY - 1) % NY
        return start(remote(block(r, h), block(to, h), kv_s.at[0], kv_r.at[to, h], peer(dy=1)))

    def minus(r, h):
        to = (r + 1) % NY
        return start(remote(block(r, h), block(to, h), kv_s.at[0], kv_r.at[to, h], peer(dy=-1)))

    def kv_arrived(r, h):
        remote(block(r, h), block(r, h), kv_s.at[0], kv_r.at[r, h], peer(dy=1)).wait_recv()

    def shared(r, h):
        dst = other(r, h)
        remote(dst, dst, sib_s.at[0], sib_r.at[r, h], peer(dc=1)).wait_recv()

    half_rows = pl.ds(pl.multiple_of(core * 64, 64), 64)

    def w_right(hop):
        rows = half_rows if hop < 3 else pl.ds(pl.multiple_of(core * 64, 64), 32)
        src, to = (NZ - hop) % NZ, NZ - 1 - hop
        start(remote(w_all.at[src, rows], w_all.at[to, rows], w_s.at[0], w_r.at[to], peer(dz=1)))

    def w_left(hop):
        rows = half_rows if hop < 3 else pl.ds(pl.multiple_of(core * 64 + 32, 32), 32)
        src, to = hop, hop + 1
        sem = w_r.at[to] if hop < 3 else w_r.at[0]
        start(remote(w_all.at[src, rows], w_all.at[to, rows], w_s.at[0], sem, peer(dz=-1)))

    def w_arrived(slot):
        if slot == 4:
            rows = pl.ds(pl.multiple_of(core * 64, 64), 32)
            dst = w_all.at[4, rows]
            remote(dst, dst, w_s.at[0], w_r.at[4], peer(dz=1)).wait_recv()
            rows = pl.ds(pl.multiple_of(core * 64 + 32, 32), 32)
            dst = w_all.at[4, rows]
            remote(dst, dst, w_s.at[0], w_r.at[0], peer(dz=1)).wait_recv()
        else:
            dst = w_all.at[slot, half_rows]
            remote(dst, dst, w_s.at[0], w_r.at[slot], peer(dz=1)).wait_recv()
        src = w_all.at[slot, half_rows]
        start(remote(src, src, ws_s.at[0], ws_r.at[slot], peer(dc=1)))

    def w_shared(slot):
        rows = pl.ds(pl.multiple_of((1 - core) * 64, 64), 64)
        dst = w_all.at[slot, rows]
        remote(dst, dst, ws_s.at[0], ws_r.at[slot], peer(dc=1)).wait_recv()

    def w_hop(hop):
        w_arrived(NZ - hop)
        w_right(hop)
        w_arrived(hop)
        w_left(hop)

    def attend(lo, rows, r, key_lo, keys, first=False):
        rs = pl.ds(lo, rows)
        ks = pl.ds(key_lo, keys)
        scores = dot_nt(qq[rs, 128:256], kv[r, ks, 0:128])
        tscores = dot_nt(qq[rs, :], kv[r, ks, 0:256])
        peak = jnp.max(scores, axis=1, keepdims=True)
        if first:
            new_top = jnp.broadcast_to(peak, (rows, 128))
        else:
            old_top = top[rs, :]
            new_top = jnp.maximum(old_top, peak)
            factor = jnp.exp2(old_top - new_top)
        top[rs, :] = new_top
        weights = jnp.exp2(scores - new_top[:, 0:1])
        mixed = weights * tscores
        sum_w, sum_m = lane_sum(weights), lane_sum(mixed)
        weights, mixed = weights.astype(BF16), mixed.astype(BF16)
        if first:
            total[rs, :] = sum_w
            spread[rs, :] = sum_m
        else:
            total[rs, :] = total[rs, :] * factor + sum_w
            spread[rs, :] = spread[rs, :] * factor + sum_m
        step = rows // 2
        for i in (0, step):
            add = dot(weights[i : i + step], kv[r, ks, 256:512])
            add_m = dot(mixed[i : i + step], kv[r, ks, 256:384])
            add_t = add[:, 128:256] + add_m
            ps = pl.ds(lo + i, step)
            if first:
                acc[ps, 0:128] = add[:, 0:128]
                acc[ps, 128:256] = add_t
            else:
                part = factor[i : i + step]
                acc[ps, 0:128] = acc[ps, 0:128] * part + add[:, 0:128]
                acc[ps, 128:256] = acc[ps, 128:256] * part + add_t

    def finish(lo):
        rs = pl.ds(lo, TOK)
        weight = jnp.sum(total[rs, :], axis=1, keepdims=True)
        inverse = 1.0 / weight
        mean = jnp.sum(spread[rs, :], axis=1, keepdims=True) * inverse
        out = acc[rs, 0:128] * inverse
        tangent = acc[rs, 128:256] * inverse - mean * out
        return out, tangent, top[rs, 0:1], weight, mean

    ld_k.wait()
    ld_rows.append(load_rows(1))
    ld_w = load(wout_hbm, w_all.at[0], 7)
    ld_q = load(wqkv_hbm.at[0], wq.at[:, 256:384], 6)
    ld_v.wait()
    project_kv(0)
    ld_w.wait()
    pl.semaphore_wait(barrier, len(friends))
    plus(0, 0)
    w_right(0)
    w_left(0)
    share(0, 0)
    project_kv(1)
    minus(0, 1)
    plus(0, 1)
    minus(0, 0)
    share(0, 1)
    ld_q.wait()
    for h in range(2):
        rows = pl.ds(TOK + h * HALF, HALF)
        flat = dot(xt[pl.ds(h * 2 * HALF, HALF), :], wq[:, 256:384])
        tflat = dot(xt[pl.ds(h * 2 * HALF + HALF, HALF), :], wq[:, 256:384])
        qq[rows, 128:256] = (flat * (SCALE * LOG2E)).astype(BF16)
        qq[rows, 0:128] = (tflat * SCALE).astype(BF16)
    q_copy = start(remote(qq.at[pl.ds(TOK, TOK)], qq.at[pl.ds(0, TOK)], q_sem.at[0], q_sem.at[1], peer(dx=1)))

    shared(0, 0)
    shared(0, 1)
    attend(TOK, TOK, 0, 0, 1024, first=True)
    kv_arrived(3, 0)
    plus(3, 0)
    share(3, 0)
    kv_arrived(1, 1)
    minus(1, 1)
    share(1, 1)
    w_hop(1)
    q_copy.wait_recv()
    attend(0, TOK, 0, 0, 1024, first=True)
    shared(3, 0)
    attend(0, 2 * TOK, 3, 0, 512)
    kv_arrived(3, 1)
    share(3, 1)
    kv_arrived(1, 0)
    share(1, 0)
    shared(1, 1)
    attend(0, 2 * TOK, 1, 512, 512)
    w_hop(2)
    shared(3, 1)
    attend(0, 2 * TOK, 3, 512, 512)
    shared(1, 0)
    attend(0, 2 * TOK, 1, 0, 512)
    kv_arrived(2, 0)
    share(2, 0)
    kv_arrived(2, 1)
    share(2, 1)
    attend(0, 2 * TOK, 2, 0, 512)
    w_hop(3)
    shared(2, 0)
    shared(2, 1)
    attend(0, TOK, 2, 512, 512)

    lane = lax.broadcasted_iota(jnp.int32, (TOK, 128), 1)

    def stat_rows(peak, weight, mean):
        stats = jnp.where(lane == 0, peak, jnp.where(lane == 1, weight, mean))
        return jnp.transpose(stats)[0:8, :]

    out, tangent, *stats = finish(0)
    part_out[:, 0:128] = out.astype(BF16)
    part_out[:, 128:256] = tangent.astype(BF16)
    stat_out[...] = stat_rows(*stats)
    stat_copy = start(remote(stat_out, stat_in, st_sem.at[0], st_sem.at[1], peer(dx=1)))

    def piece(k):
        return pl.ds(pl.multiple_of(lax.rem(z + k, NZ) * PIECE, PIECE), PIECE)

    part_copies = {}
    for k in ORDER:
        rows = piece(k)
        part_copies[k] = start(remote(part_out.at[rows], part_in.at[rows], p_s.at[0], p_r.at[k], peer(dx=1)))
    attend(TOK, TOK, 2, 512, 512)
    out, tangent, *stats = finish(TOK)
    own_part[:, 0:128] = out
    own_part[:, 128:256] = tangent
    own = stat_rows(*stats)
    stat_copy.wait_recv()
    peak, weight, mean = own[0:1, :], own[1:2, :], own[2:3, :]
    peak2, weight2, mean2 = stat_in[0:1, :], stat_in[1:2, :], stat_in[2:3, :]
    high = jnp.maximum(peak, peak2)
    mass = weight * jnp.exp2(peak - high)
    mass2 = weight2 * jnp.exp2(peak2 - high)
    inverse = 1.0 / (mass + mass2)
    p1, p2 = mass * inverse, mass2 * inverse
    p3 = p1 * p2 * (mean - mean2)
    columns = jnp.transpose(jnp.concatenate([p1, p2, p3, jnp.zeros((125, TOK), F32)], axis=0))
    for i in range(3):
        coef[i] = jnp.broadcast_to(columns[:, i : i + 1], (TOK, 128))

    a_copies = {}
    for k in ORDER:
        rows = piece(k)
        if k == 6:
            w_arrived(4)
        part_copies[k].wait_recv()
        o1, u1 = own_part[rows, 0:128], own_part[rows, 128:256]
        o2, u2 = part_in[rows, 0:128].astype(F32), part_in[rows, 128:256].astype(F32)
        c1, c2, c3 = coef[0, rows, :], coef[1, rows, :], coef[2, rows, :]
        merged = (c1 * o1 + c2 * o2).astype(BF16)
        tmerged = (c1 * u1 + c2 * u2 + c3 * (o1 - o2)).astype(BF16)
        if k == 0:
            a_in[0:PIECE, 0:128] = merged
            a_in[PIECE : 2 * PIECE, 0:128] = tmerged
        else:
            a_out[k, 0:PIECE, :] = merged
            a_out[k, PIECE : 2 * PIECE, :] = tmerged
            back = NZ - k
            dst = a_in.at[:, back * 128 : back * 128 + 128]
            a_copies[k] = start(remote(a_out.at[k], dst, a_s.at[0], a_r.at[back], peer(dz=k)))

    for slot in range(1, NZ):
        w_shared(slot)
    for k in range(1, NZ):
        a_copies[k].wait_recv()

    def columns(b, k):
        column = (lax.rem(xh + b, NH) * NZ + lax.rem(z + k, NZ)) * 128
        return w_all[:, :, pl.ds(pl.multiple_of(column, 128), 128)].reshape(NZ * 128, 128)

    g_copies = {}
    for k in ORDER:
        both = dot(a_in[...], jnp.concatenate([columns(1, k), columns(0, k)], axis=1))
        g_out[k] = both[:, 0:128].astype(BF16)
        g_copies[k] = start(remote(g_out.at[k], g_in.at[k], g_s.at[0], g_r.at[k], peer(dh=1)))
        g_own[k] = both[:, 128:256]
    for k in ORDER:
        g_copies[k].wait_recv()
        term = (g_own[k] + g_in[k].astype(F32)).astype(BF16)
        if k == 0:
            out_ref[piece(0), :] = term[0:PIECE]
            tout_ref[piece(0), :] = term[PIECE : 2 * PIECE]
        else:
            f_out[k] = term
            start(remote(f_out.at[k], f_in.at[NZ - k], f_s.at[0], f_r.at[NZ - k], peer(dz=k)))
    sent(kv_s.at[0], xt.at[pl.ds(0, 6 * 64)])
    sent(sib_s.at[0], xt.at[pl.ds(0, 8 * 64)])
    sent(w_s.at[0], xt.at[pl.ds(0, 7 * 64)])
    sent(ws_s.at[0], xt.at[pl.ds(0, 7 * 64)])
    sent(p_s.at[0], part_out)
    sent(a_s.at[0], a_out.at[pl.ds(1, NZ - 1)])
    sent(g_s.at[0], g_out)
    q_copy.wait_send()
    stat_copy.wait_send()
    for k in ORDER:
        if k != 0:
            remote(f_in.at[k], f_in.at[k], f_s.at[0], f_r.at[k], peer(dz=k)).wait_recv()
            out_ref[piece(k), :] = f_in[k, 0:PIECE]
            tout_ref[piece(k), :] = f_in[k, PIECE : 2 * PIECE]
    sent(f_s.at[0], f_out.at[pl.ds(1, NZ - 1)])


def local(inputs, tangents, w_qkv, w_out):
    dma = pltpu.SemaphoreType.DMA
    vmem = pltpu.VMEM
    result = pl.pallas_call(
        kernel,
        name="tangent_attention",
        out_shape=pltpu.VMEM((2 * TOK, 128), BF16),
        in_specs=[pl.BlockSpec(memory_space=pl.ANY)] * 4,
        out_specs=pl.BlockSpec(memory_space=pltpu.VMEM),
        scratch_shapes=[
            vmem((2 * TOK, D), BF16),
            vmem((D, 384), BF16),
            vmem((NY, 1024, 512), BF16),
            vmem((2 * TOK, 256), BF16),
            vmem((2 * TOK, 256), F32),
            vmem((2 * TOK, 128), F32),
            vmem((2 * TOK, 128), F32),
            vmem((2 * TOK, 128), F32),
            vmem((TOK, 256), BF16),
            vmem((TOK, 256), BF16),
            vmem((8, TOK), F32),
            vmem((8, TOK), F32),
            vmem((TOK, 256), F32),
            vmem((3, TOK, 128), F32),
            vmem((NZ, 128, 128), BF16),
            vmem((128, NZ * 128), BF16),
            vmem((NZ, 128, D), BF16),
            vmem((NZ, 128, 128), BF16),
            vmem((NZ, 128, 128), BF16),
            vmem((NZ, 128, 128), F32),
            vmem((NZ, 128, 128), BF16),
            vmem((NZ, 128, 128), BF16),
            dma((8,)),
            dma((1,)),
            dma((NY, 2)),
            dma((1,)),
            dma((NY, 2)),
            dma((2,)),
            dma((1,)),
            dma((8,)),
            dma((1,)),
            dma((8,)),
            dma((1,)),
            dma((8,)),
            dma((2,)),
            dma((1,)),
            dma((8,)),
            dma((1,)),
            dma((8,)),
            dma((1,)),
            dma((8,)),
        ],
        compiler_params=pltpu.CompilerParams(
            collective_id=0, has_side_effects=True, vmem_limit_bytes=58 * 2**20
        ),
    )(inputs, tangents, w_qkv, w_out)
    return result[:TOK], result[TOK:]


def solution(mesh):
    return jax.shard_map(
        local,
        mesh=mesh,
        in_specs=(P("ctx", None), P("ctx", None), P(None, None, "head"), P("head", None)),
        out_specs=(P("ctx", "head"), P("ctx", "head")),
        check_vma=False,
    )
```

```python
import functools
import math

import jax
import jax.numpy as jnp
from jax import lax
from jax.experimental import pallas as pl
from jax.experimental.pallas import tpu as pltpu
from jax.sharding import PartitionSpec as P

F32 = jnp.float32
BF16 = jnp.bfloat16
MESH = pl.DeviceIdType.MESH
HD = 128
D = 2048
TOK = 512
HALF = TOK // 2
NY, NX, NC = 4, 2, 2
NH, NZ = 2, 8
PIECE = TOK // NZ
LOG2E = math.log2(math.e)
LN2 = math.log(2.0)
SCALE = HD ** (-0.5)
ORDER = (3, 5, 4, 2, 6, 1, 7, 0)


def dot(a, b):
    return jnp.dot(a, b, preferred_element_type=F32)


def dot_nt(a, b):
    return lax.dot_general(a, b, (((1,), (1,)), ((), ())), preferred_element_type=F32)


def lane_sum(value):
    parts = [value[:, i : i + 128] for i in range(0, value.shape[1], 128)]
    return functools.reduce(lambda a, b: a + b, parts)


def kernel(
    x_hbm, t_hbm, wqkv_hbm, wout_hbm, both_ref,
    xt, wq, kv, qq, acc, top, total, spread,
    part_out, part_in, stat_out, stat_in, own_part, coef,
    a_out, a_in, w_all, g_out, g_in, g_own, f_out, f_in,
    ld, kv_s, kv_r, sib_s, sib_r, q_sem, w_s, w_r, ws_s, ws_r,
    p_s, p_r, st_sem, a_s, a_r, g_s, g_r, f_s, f_r,
):
    out_ref, tout_ref = both_ref.at[pl.ds(0, TOK)], both_ref.at[pl.ds(TOK, TOK)]
    ctx = lax.axis_index("ctx")
    head = lax.axis_index("head")
    y, x, core = ctx // 4, (ctx // 2) % 2, ctx % 2
    xh, z = head // 8, head % 8

    def peer(dy=0, dx=0, dc=0, dh=0, dz=0):
        ny = lax.rem(y + (dy + NY), NY)
        nx = lax.rem(x + dx, NX)
        nc = lax.rem(core + dc, NC)
        nh = lax.rem(xh + dh, NH)
        nz = lax.rem(z + (dz + NZ), NZ)
        return ((ny * NX + nx) * NC + nc, nh * NZ + nz)

    def remote(src, dst, send, recv, device):
        return pltpu.make_async_remote_copy(
            src_ref=src, dst_ref=dst, send_sem=send, recv_sem=recv, device_id=device, device_id_type=MESH
        )

    friends = [peer(dc=1), peer(dx=1), peer(dy=1), peer(dy=-1)]
    friends += [peer(dz=k) for k in range(1, NZ)] + [peer(dh=1)]
    barrier = pltpu.get_barrier_semaphore()
    for friend in friends:
        pl.semaphore_signal(barrier, inc=1, device_id=friend, device_id_type=MESH)

    def load(src, dst, index):
        copy = pltpu.make_async_copy(src, dst, ld.at[index])
        copy.start()
        return copy

    def load_rows(h):
        rows = pl.ds(h * HALF, HALF)
        first = load(x_hbm.at[rows], xt.at[pl.ds(2 * h * HALF, HALF)], 2 + h)
        return first, load(t_hbm.at[rows], xt.at[pl.ds(2 * h * HALF + HALF, HALF)], 4 + h)

    ld_k = load(wqkv_hbm.at[1], wq.at[:, 0:128], 0)
    ld_v = load(wqkv_hbm.at[2], wq.at[:, 128:256], 1)
    ld_rows = [load_rows(0)]

    def start(copy):
        copy.start()
        return copy

    def sent(sem, src):
        remote(src, src, sem, q_sem.at[1], peer(dc=1)).wait_send()

    def project_kv(h):
        rows = pl.ds(h * 2 * HALF, HALF)
        ld_rows[h][0].wait()
        ld_rows[h][1].wait()
        flat = dot(xt[pl.ds(h * 2 * HALF, HALF), :], wq[:, 0:256])
        tflat = dot(xt[pl.ds(h * 2 * HALF + HALF, HALF), :], wq[:, 0:256])
        kv[0, rows, 0:128] = flat[:, 0:128].astype(BF16)
        kv[0, rows, 256:384] = flat[:, 128:256].astype(BF16)
        kv[0, rows, 128:256] = (tflat[:, 0:128] * LN2).astype(BF16)
        kv[0, rows, 384:512] = tflat[:, 128:256].astype(BF16)

    def block(r, h):
        return kv.at[r, pl.ds(h * HALF if r == 2 else h * 2 * HALF, HALF)]

    def other(r, h):
        return kv.at[r, pl.ds(h * HALF + 2 * HALF if r == 2 else h * 2 * HALF + HALF, HALF)]

    def share(r, h):
        dst = other(r, h)
        return start(remote(block(r, h), dst, sib_s.at[0], sib_r.at[r, h], peer(dc=1)))

    def plus(r, h):
        to = (r + NY - 1) % NY
        return start(remote(block(r, h), block(to, h), kv_s.at[0], kv_r.at[to, h], peer(dy=1)))

    def minus(r, h):
        to = (r + 1) % NY
        return start(remote(block(r, h), block(to, h), kv_s.at[0], kv_r.at[to, h], peer(dy=-1)))

    def kv_arrived(r, h):
        remote(block(r, h), block(r, h), kv_s.at[0], kv_r.at[r, h], peer(dy=1)).wait_recv()

    def shared(r, h):
        dst = other(r, h)
        remote(dst, dst, sib_s.at[0], sib_r.at[r, h], peer(dc=1)).wait_recv()

    half_rows = pl.ds(pl.multiple_of(core * 64, 64), 64)

    def w_right(hop):
        rows = half_rows if hop < 3 else pl.ds(pl.multiple_of(core * 64, 64), 32)
        src, to = (NZ - hop) % NZ, NZ - 1 - hop
        start(remote(w_all.at[src, rows], w_all.at[to, rows], w_s.at[0], w_r.at[to], peer(dz=1)))

    def w_left(hop):
        rows = half_rows if hop < 3 else pl.ds(pl.multiple_of(core * 64 + 32, 32), 32)
        src, to = hop, hop + 1
        sem = w_r.at[to] if hop < 3 else w_r.at[0]
        start(remote(w_all.at[src, rows], w_all.at[to, rows], w_s.at[0], sem, peer(dz=-1)))

    def w_arrived(slot):
        if slot == 4:
            rows = pl.ds(pl.multiple_of(core * 64, 64), 32)
            dst = w_all.at[4, rows]
            remote(dst, dst, w_s.at[0], w_r.at[4], peer(dz=1)).wait_recv()
            rows = pl.ds(pl.multiple_of(core * 64 + 32, 32), 32)
            dst = w_all.at[4, rows]
            remote(dst, dst, w_s.at[0], w_r.at[0], peer(dz=1)).wait_recv()
        else:
            dst = w_all.at[slot, half_rows]
            remote(dst, dst, w_s.at[0], w_r.at[slot], peer(dz=1)).wait_recv()
        src = w_all.at[slot, half_rows]
        start(remote(src, src, ws_s.at[0], ws_r.at[slot], peer(dc=1)))

    def w_shared(slot):
        rows = pl.ds(pl.multiple_of((1 - core) * 64, 64), 64)
        dst = w_all.at[slot, rows]
        remote(dst, dst, ws_s.at[0], ws_r.at[slot], peer(dc=1)).wait_recv()

    def w_hop(hop):
        w_arrived(NZ - hop)
        w_right(hop)
        w_arrived(hop)
        w_left(hop)

    def attend(lo, rows, r, key_lo, keys, first=False):
        rs = pl.ds(lo, rows)
        ks = pl.ds(key_lo, keys)
        scores = dot_nt(qq[rs, 128:256], kv[r, ks, 0:128])
        tscores = dot_nt(qq[rs, :], kv[r, ks, 0:256])
        peak = jnp.max(scores, axis=1, keepdims=True)
        if first:
            new_top = jnp.broadcast_to(peak, (rows, 128))
        else:
            old_top = top[rs, :]
            new_top = jnp.maximum(old_top, peak)
            factor = jnp.exp2(old_top - new_top)
        top[rs, :] = new_top
        weights = jnp.exp2(scores - new_top[:, 0:1])
        mixed = weights * tscores
        sum_w, sum_m = lane_sum(weights), lane_sum(mixed)
        weights, mixed = weights.astype(BF16), mixed.astype(BF16)
        if first:
            total[rs, :] = sum_w
            spread[rs, :] = sum_m
        else:
            total[rs, :] = total[rs, :] * factor + sum_w
            spread[rs, :] = spread[rs, :] * factor + sum_m
        step = rows // 2
        for i in (0, step):
            add = dot(weights[i : i + step], kv[r, ks, 256:512])
            add_m = dot(mixed[i : i + step], kv[r, ks, 256:384])
            add_t = add[:, 128:256] + add_m
            ps = pl.ds(lo + i, step)
            if first:
                acc[ps, 0:128] = add[:, 0:128]
                acc[ps, 128:256] = add_t
            else:
                part = factor[i : i + step]
                acc[ps, 0:128] = acc[ps, 0:128] * part + add[:, 0:128]
                acc[ps, 128:256] = acc[ps, 128:256] * part + add_t

    def finish(lo):
        rs = pl.ds(lo, TOK)
        weight = jnp.sum(total[rs, :], axis=1, keepdims=True)
        inverse = 1.0 / weight
        mean = jnp.sum(spread[rs, :], axis=1, keepdims=True) * inverse
        out = acc[rs, 0:128] * inverse
        tangent = acc[rs, 128:256] * inverse - mean * out
        return out, tangent, top[rs, 0:1], weight, mean

    ld_k.wait()
    ld_rows.append(load_rows(1))
    ld_w = load(wout_hbm, w_all.at[0], 7)
    ld_q = load(wqkv_hbm.at[0], wq.at[:, 256:384], 6)
    ld_v.wait()
    project_kv(0)
    ld_w.wait()
    pl.semaphore_wait(barrier, len(friends))
    plus(0, 0)
    w_right(0)
    w_left(0)
    share(0, 0)
    project_kv(1)
    minus(0, 1)
    plus(0, 1)
    minus(0, 0)
    share(0, 1)
    ld_q.wait()
    for h in range(2):
        rows = pl.ds(TOK + h * HALF, HALF)
        flat = dot(xt[pl.ds(h * 2 * HALF, HALF), :], wq[:, 256:384])
        tflat = dot(xt[pl.ds(h * 2 * HALF + HALF, HALF), :], wq[:, 256:384])
        qq[rows, 128:256] = (flat * (SCALE * LOG2E)).astype(BF16)
        qq[rows, 0:128] = (tflat * SCALE).astype(BF16)
    q_copy = start(remote(qq.at[pl.ds(TOK, TOK)], qq.at[pl.ds(0, TOK)], q_sem.at[0], q_sem.at[1], peer(dx=1)))

    shared(0, 0)
    shared(0, 1)
    attend(TOK, TOK, 0, 0, 1024, first=True)
    kv_arrived(3, 0)
    plus(3, 0)
    share(3, 0)
    kv_arrived(1, 1)
    minus(1, 1)
    share(1, 1)
    w_hop(1)
    q_copy.wait_recv()
    attend(0, TOK, 0, 0, 1024, first=True)
    shared(3, 0)
    attend(0, 2 * TOK, 3, 0, 512)
    kv_arrived(3, 1)
    share(3, 1)
    kv_arrived(1, 0)
    share(1, 0)
    shared(1, 1)
    attend(0, 2 * TOK, 1, 512, 512)
    w_hop(2)
    shared(3, 1)
    attend(0, 2 * TOK, 3, 512, 512)
    shared(1, 0)
    attend(0, 2 * TOK, 1, 0, 512)
    kv_arrived(2, 0)
    share(2, 0)
    kv_arrived(2, 1)
    share(2, 1)
    attend(0, 2 * TOK, 2, 0, 512)
    w_hop(3)
    shared(2, 0)
    shared(2, 1)
    attend(0, TOK, 2, 512, 512)

    lane = lax.broadcasted_iota(jnp.int32, (TOK, 128), 1)

    def stat_rows(peak, weight, mean):
        stats = jnp.where(lane == 0, peak, jnp.where(lane == 1, weight, mean))
        return jnp.transpose(stats)[0:8, :]

    out, tangent, *stats = finish(0)
    part_out[:, 0:128] = out.astype(BF16)
    part_out[:, 128:256] = tangent.astype(BF16)
    stat_out[...] = stat_rows(*stats)
    stat_copy = start(remote(stat_out, stat_in, st_sem.at[0], st_sem.at[1], peer(dx=1)))

    def piece(k):
        return pl.ds(pl.multiple_of(lax.rem(z + k, NZ) * PIECE, PIECE), PIECE)

    part_copies = {}
    for k in ORDER:
        rows = piece(k)
        part_copies[k] = start(remote(part_out.at[rows], part_in.at[rows], p_s.at[0], p_r.at[k], peer(dx=1)))
    attend(TOK, TOK, 2, 512, 512)
    out, tangent, *stats = finish(TOK)
    own_part[:, 0:128] = out
    own_part[:, 128:256] = tangent
    own = stat_rows(*stats)
    stat_copy.wait_recv()
    peak, weight, mean = own[0:1, :], own[1:2, :], own[2:3, :]
    peak2, weight2, mean2 = stat_in[0:1, :], stat_in[1:2, :], stat_in[2:3, :]
    high = jnp.maximum(peak, peak2)
    mass = weight * jnp.exp2(peak - high)
    mass2 = weight2 * jnp.exp2(peak2 - high)
    inverse = 1.0 / (mass + mass2)
    p1, p2 = mass * inverse, mass2 * inverse
    p3 = p1 * p2 * (mean - mean2)
    columns = jnp.transpose(jnp.concatenate([p1, p2, p3, jnp.zeros((125, TOK), F32)], axis=0))
    for i in range(3):
        coef[i] = jnp.broadcast_to(columns[:, i : i + 1], (TOK, 128))

    a_copies = {}
    for k in ORDER:
        rows = piece(k)
        if k == 6:
            w_arrived(4)
        part_copies[k].wait_recv()
        o1, u1 = own_part[rows, 0:128], own_part[rows, 128:256]
        o2, u2 = part_in[rows, 0:128].astype(F32), part_in[rows, 128:256].astype(F32)
        c1, c2, c3 = coef[0, rows, :], coef[1, rows, :], coef[2, rows, :]
        merged = (c1 * o1 + c2 * o2).astype(BF16)
        tmerged = (c1 * u1 + c2 * u2 + c3 * (o1 - o2)).astype(BF16)
        if k == 0:
            a_in[0:PIECE, 0:128] = merged
            a_in[PIECE : 2 * PIECE, 0:128] = tmerged
        else:
            a_out[k, 0:PIECE, :] = merged
            a_out[k, PIECE : 2 * PIECE, :] = tmerged
            back = NZ - k
            dst = a_in.at[:, back * 128 : back * 128 + 128]
            a_copies[k] = start(remote(a_out.at[k], dst, a_s.at[0], a_r.at[back], peer(dz=k)))

    for slot in range(1, NZ):
        w_shared(slot)
    for k in range(1, NZ):
        a_copies[k].wait_recv()

    def columns(b, k):
        column = (lax.rem(xh + b, NH) * NZ + lax.rem(z + k, NZ)) * 128
        return w_all[:, :, pl.ds(pl.multiple_of(column, 128), 128)].reshape(NZ * 128, 128)

    g_copies = {}
    for k in ORDER:
        both = dot(a_in[...], jnp.concatenate([columns(1, k), columns(0, k)], axis=1))
        g_out[k] = both[:, 0:128].astype(BF16)
        g_copies[k] = start(remote(g_out.at[k], g_in.at[k], g_s.at[0], g_r.at[k], peer(dh=1)))
        g_own[k] = both[:, 128:256]
    for k in ORDER:
        g_copies[k].wait_recv()
        term = (g_own[k] + g_in[k].astype(F32)).astype(BF16)
        if k == 0:
            out_ref[piece(0), :] = term[0:PIECE]
            tout_ref[piece(0), :] = term[PIECE : 2 * PIECE]
        else:
            f_out[k] = term
            start(remote(f_out.at[k], f_in.at[NZ - k], f_s.at[0], f_r.at[NZ - k], peer(dz=k)))
    sent(kv_s.at[0], xt.at[pl.ds(0, 6 * 64)])
    sent(sib_s.at[0], xt.at[pl.ds(0, 8 * 64)])
    sent(w_s.at[0], xt.at[pl.ds(0, 7 * 64)])
    sent(ws_s.at[0], xt.at[pl.ds(0, 7 * 64)])
    sent(p_s.at[0], part_out)
    sent(a_s.at[0], a_out.at[pl.ds(1, NZ - 1)])
    sent(g_s.at[0], g_out)
    q_copy.wait_send()
    stat_copy.wait_send()
    for k in ORDER:
        if k != 0:
            remote(f_in.at[k], f_in.at[k], f_s.at[0], f_r.at[k], peer(dz=k)).wait_recv()
            out_ref[piece(k), :] = f_in[k, 0:PIECE]
            tout_ref[piece(k), :] = f_in[k, PIECE : 2 * PIECE]
    sent(f_s.at[0], f_out.at[pl.ds(1, NZ - 1)])


def local(inputs, tangents, w_qkv, w_out):
    dma = pltpu.SemaphoreType.DMA
    vmem = pltpu.VMEM
    result = pl.pallas_call(
        kernel,
        name="tangent_attention",
        out_shape=pltpu.VMEM((2 * TOK, 128), BF16),
        in_specs=[pl.BlockSpec(memory_space=pl.ANY)] * 4,
        out_specs=pl.BlockSpec(memory_space=pltpu.VMEM),
        scratch_shapes=[
            vmem((2 * TOK, D), BF16),
            vmem((D, 384), BF16),
            vmem((NY, 1024, 512), BF16),
            vmem((2 * TOK, 256), BF16),
            vmem((2 * TOK, 256), F32),
            vmem((2 * TOK, 128), F32),
            vmem((2 * TOK, 128), F32),
            vmem((2 * TOK, 128), F32),
            vmem((TOK, 256), BF16),
            vmem((TOK, 256), BF16),
            vmem((8, TOK), F32),
            vmem((8, TOK), F32),
            vmem((TOK, 256), F32),
            vmem((3, TOK, 128), F32),
            vmem((NZ, 128, 128), BF16),
            vmem((128, NZ * 128), BF16),
            vmem((NZ, 128, D), BF16),
            vmem((NZ, 128, 128), BF16),
            vmem((NZ, 128, 128), BF16),
            vmem((NZ, 128, 128), F32),
            vmem((NZ, 128, 128), BF16),
            vmem((NZ, 128, 128), BF16),
            dma((8,)),
            dma((1,)),
            dma((NY, 2)),
            dma((1,)),
            dma((NY, 2)),
            dma((2,)),
            dma((1,)),
            dma((8,)),
            dma((1,)),
            dma((8,)),
            dma((1,)),
            dma((8,)),
            dma((2,)),
            dma((1,)),
            dma((8,)),
            dma((1,)),
            dma((8,)),
            dma((1,)),
            dma((8,)),
        ],
        compiler_params=pltpu.CompilerParams(
            collective_id=0, has_side_effects=True, vmem_limit_bytes=58 * 2**20
        ),
    )(inputs, tangents, w_qkv, w_out)
    return result[:TOK], result[TOK:]


def solution(mesh):
    return jax.shard_map(
        local,
        mesh=mesh,
        in_specs=(P("ctx", None), P("ctx", None), P(None, None, "head"), P("head", None)),
        out_specs=(P("ctx", "head"), P("ctx", "head")),
        check_vma=False,
    )
```

```python
import functools
import math

import jax
import jax.numpy as jnp
from jax import lax
from jax.experimental import pallas as pl
from jax.experimental.pallas import tpu as pltpu
from jax.sharding import PartitionSpec as P

F32 = jnp.float32
BF16 = jnp.bfloat16
MESH = pl.DeviceIdType.MESH
HD = 128
D = 2048
TOK = 512
HALF = TOK // 2
NY, NX, NC = 4, 2, 2
NH, NZ = 2, 8
PIECE = TOK // NZ
LOG2E = math.log2(math.e)
LN2 = math.log(2.0)
SCALE = HD ** (-0.5)
ORDER = (3, 5, 4, 2, 6, 1, 7, 0)


def dot(a, b):
    return jnp.dot(a, b, preferred_element_type=F32)


def dot_nt(a, b):
    return lax.dot_general(a, b, (((1,), (1,)), ((), ())), preferred_element_type=F32)


def lane_sum(value):
    parts = [value[:, i : i + 128] for i in range(0, value.shape[1], 128)]
    return functools.reduce(lambda a, b: a + b, parts)


def kernel(
    x_hbm, t_hbm, wqkv_hbm, wout_hbm, both_ref,
    xt, wq, kv, qq, acc, top, total, spread,
    part_out, part_in, stat_out, stat_in, own_part, coef,
    a_out, a_in, w_all, g_out, g_in, g_own, f_out, f_in,
    ld, kv_s, kv_r, sib_s, sib_r, q_sem, w_s, w_r, ws_s, ws_r,
    p_s, p_r, st_sem, a_s, a_r, g_s, g_r, f_s, f_r,
):
    out_ref, tout_ref = both_ref.at[pl.ds(0, TOK)], both_ref.at[pl.ds(TOK, TOK)]
    ctx = lax.axis_index("ctx")
    head = lax.axis_index("head")
    y, x, core = ctx // 4, (ctx // 2) % 2, ctx % 2
    xh, z = head // 8, head % 8

    def peer(dy=0, dx=0, dc=0, dh=0, dz=0):
        ny = lax.rem(y + (dy + NY), NY)
        nx = lax.rem(x + dx, NX)
        nc = lax.rem(core + dc, NC)
        nh = lax.rem(xh + dh, NH)
        nz = lax.rem(z + (dz + NZ), NZ)
        return ((ny * NX + nx) * NC + nc, nh * NZ + nz)

    def remote(src, dst, send, recv, device):
        return pltpu.make_async_remote_copy(
            src_ref=src, dst_ref=dst, send_sem=send, recv_sem=recv, device_id=device, device_id_type=MESH
        )

    friends = [peer(dc=1), peer(dx=1), peer(dy=1), peer(dy=-1)]
    friends += [peer(dz=k) for k in range(1, NZ)] + [peer(dh=1)]
    barrier = pltpu.get_barrier_semaphore()
    for friend in friends:
        pl.semaphore_signal(barrier, inc=1, device_id=friend, device_id_type=MESH)

    def load(src, dst, index):
        copy = pltpu.make_async_copy(src, dst, ld.at[index])
        copy.start()
        return copy

    def load_rows(h):
        rows = pl.ds(h * HALF, HALF)
        first = load(x_hbm.at[rows], xt.at[pl.ds(2 * h * HALF, HALF)], 2 + h)
        return first, load(t_hbm.at[rows], xt.at[pl.ds(2 * h * HALF + HALF, HALF)], 4 + h)

    ld_k = load(wqkv_hbm.at[1], wq.at[:, 0:128], 0)
    ld_v = load(wqkv_hbm.at[2], wq.at[:, 128:256], 1)
    ld_rows = [load_rows(0)]

    def start(copy):
        copy.start()
        return copy

    def sent(sem, src):
        remote(src, src, sem, q_sem.at[1], peer(dc=1)).wait_send()

    def project_kv(h):
        rows = pl.ds(h * 2 * HALF, HALF)
        ld_rows[h][0].wait()
        ld_rows[h][1].wait()
        flat = dot(xt[pl.ds(h * 2 * HALF, HALF), :], wq[:, 0:256])
        tflat = dot(xt[pl.ds(h * 2 * HALF + HALF, HALF), :], wq[:, 0:256])
        kv[0, rows, 0:128] = flat[:, 0:128].astype(BF16)
        kv[0, rows, 256:384] = flat[:, 128:256].astype(BF16)
        kv[0, rows, 128:256] = (tflat[:, 0:128] * LN2).astype(BF16)
        kv[0, rows, 384:512] = tflat[:, 128:256].astype(BF16)

    def block(r, h):
        return kv.at[r, pl.ds(h * HALF if r == 2 else h * 2 * HALF, HALF)]

    def other(r, h):
        return kv.at[r, pl.ds(h * HALF + 2 * HALF if r == 2 else h * 2 * HALF + HALF, HALF)]

    def share(r, h):
        dst = other(r, h)
        return start(remote(block(r, h), dst, sib_s.at[0], sib_r.at[r, h], peer(dc=1)))

    def plus(r, h):
        to = (r + NY - 1) % NY
        return start(remote(block(r, h), block(to, h), kv_s.at[0], kv_r.at[to, h], peer(dy=1)))

    def minus(r, h):
        to = (r + 1) % NY
        return start(remote(block(r, h), block(to, h), kv_s.at[0], kv_r.at[to, h], peer(dy=-1)))

    def kv_arrived(r, h):
        remote(block(r, h), block(r, h), kv_s.at[0], kv_r.at[r, h], peer(dy=1)).wait_recv()

    def shared(r, h):
        dst = other(r, h)
        remote(dst, dst, sib_s.at[0], sib_r.at[r, h], peer(dc=1)).wait_recv()

    half_rows = pl.ds(pl.multiple_of(core * 64, 64), 64)

    def w_right(hop):
        rows = half_rows if hop < 3 else pl.ds(pl.multiple_of(core * 64, 64), 32)
        src, to = (NZ - hop) % NZ, NZ - 1 - hop
        start(remote(w_all.at[src, rows], w_all.at[to, rows], w_s.at[0], w_r.at[to], peer(dz=1)))

    def w_left(hop):
        rows = half_rows if hop < 3 else pl.ds(pl.multiple_of(core * 64 + 32, 32), 32)
        src, to = hop, hop + 1
        sem = w_r.at[to] if hop < 3 else w_r.at[0]
        start(remote(w_all.at[src, rows], w_all.at[to, rows], w_s.at[0], sem, peer(dz=-1)))

    def w_arrived(slot):
        if slot == 4:
            rows = pl.ds(pl.multiple_of(core * 64, 64), 32)
            dst = w_all.at[4, rows]
            remote(dst, dst, w_s.at[0], w_r.at[4], peer(dz=1)).wait_recv()
            rows = pl.ds(pl.multiple_of(core * 64 + 32, 32), 32)
            dst = w_all.at[4, rows]
            remote(dst, dst, w_s.at[0], w_r.at[0], peer(dz=1)).wait_recv()
        else:
            dst = w_all.at[slot, half_rows]
            remote(dst, dst, w_s.at[0], w_r.at[slot], peer(dz=1)).wait_recv()
        src = w_all.at[slot, half_rows]
        start(remote(src, src, ws_s.at[0], ws_r.at[slot], peer(dc=1)))

    def w_shared(slot):
        rows = pl.ds(pl.multiple_of((1 - core) * 64, 64), 64)
        dst = w_all.at[slot, rows]
        remote(dst, dst, ws_s.at[0], ws_r.at[slot], peer(dc=1)).wait_recv()

    def w_hop(hop):
        w_arrived(NZ - hop)
        w_right(hop)
        w_arrived(hop)
        w_left(hop)

    def attend(lo, rows, r, key_lo, keys, first=False):
        rs = pl.ds(lo, rows)
        ks = pl.ds(key_lo, keys)
        scores = dot_nt(qq[rs, 128:256], kv[r, ks, 0:128])
        tscores = dot_nt(qq[rs, :], kv[r, ks, 0:256])
        peak = jnp.max(scores, axis=1, keepdims=True)
        if first:
            new_top = jnp.broadcast_to(peak, (rows, 128))
        else:
            old_top = top[rs, :]
            new_top = jnp.maximum(old_top, peak)
            factor = jnp.exp2(old_top - new_top)
        top[rs, :] = new_top
        weights = jnp.exp2(scores - new_top[:, 0:1])
        mixed = weights * tscores
        sum_w, sum_m = lane_sum(weights), lane_sum(mixed)
        weights, mixed = weights.astype(BF16), mixed.astype(BF16)
        if first:
            total[rs, :] = sum_w
            spread[rs, :] = sum_m
        else:
            total[rs, :] = total[rs, :] * factor + sum_w
            spread[rs, :] = spread[rs, :] * factor + sum_m
        step = rows // 2
        for i in (0, step):
            add = dot(weights[i : i + step], kv[r, ks, 256:512])
            add_m = dot(mixed[i : i + step], kv[r, ks, 256:384])
            add_t = add[:, 128:256] + add_m
            ps = pl.ds(lo + i, step)
            if first:
                acc[ps, 0:128] = add[:, 0:128]
                acc[ps, 128:256] = add_t
            else:
                part = factor[i : i + step]
                acc[ps, 0:128] = acc[ps, 0:128] * part + add[:, 0:128]
                acc[ps, 128:256] = acc[ps, 128:256] * part + add_t

    def finish(lo):
        rs = pl.ds(lo, TOK)
        weight = jnp.sum(total[rs, :], axis=1, keepdims=True)
        inverse = 1.0 / weight
        mean = jnp.sum(spread[rs, :], axis=1, keepdims=True) * inverse
        out = acc[rs, 0:128] * inverse
        tangent = acc[rs, 128:256] * inverse - mean * out
        return out, tangent, top[rs, 0:1], weight, mean

    ld_k.wait()
    ld_rows.append(load_rows(1))
    ld_w = load(wout_hbm, w_all.at[0], 7)
    ld_q = load(wqkv_hbm.at[0], wq.at[:, 256:384], 6)
    ld_v.wait()
    project_kv(0)
    ld_w.wait()
    pl.semaphore_wait(barrier, len(friends))
    plus(0, 0)
    w_right(0)
    w_left(0)
    share(0, 0)
    project_kv(1)
    minus(0, 1)
    plus(0, 1)
    minus(0, 0)
    share(0, 1)
    ld_q.wait()
    for h in range(2):
        rows = pl.ds(TOK + h * HALF, HALF)
        flat = dot(xt[pl.ds(h * 2 * HALF, HALF), :], wq[:, 256:384])
        tflat = dot(xt[pl.ds(h * 2 * HALF + HALF, HALF), :], wq[:, 256:384])
        qq[rows, 128:256] = (flat * (SCALE * LOG2E)).astype(BF16)
        qq[rows, 0:128] = (tflat * SCALE).astype(BF16)
    q_copy = start(remote(qq.at[pl.ds(TOK, TOK)], qq.at[pl.ds(0, TOK)], q_sem.at[0], q_sem.at[1], peer(dx=1)))

    shared(0, 0)
    shared(0, 1)
    attend(TOK, TOK, 0, 0, 1024, first=True)
    kv_arrived(3, 0)
    plus(3, 0)
    share(3, 0)
    kv_arrived(1, 1)
    minus(1, 1)
    share(1, 1)
    w_hop(1)
    q_copy.wait_recv()
    attend(0, TOK, 0, 0, 1024, first=True)
    shared(3, 0)
    attend(0, 2 * TOK, 3, 0, 512)
    kv_arrived(3, 1)
    share(3, 1)
    kv_arrived(1, 0)
    share(1, 0)
    shared(1, 1)
    attend(0, 2 * TOK, 1, 512, 512)
    w_hop(2)
    shared(3, 1)
    attend(0, 2 * TOK, 3, 512, 512)
    shared(1, 0)
    attend(0, 2 * TOK, 1, 0, 512)
    kv_arrived(2, 0)
    share(2, 0)
    kv_arrived(2, 1)
    share(2, 1)
    attend(0, 2 * TOK, 2, 0, 512)
    w_hop(3)
    shared(2, 0)
    shared(2, 1)
    attend(0, TOK, 2, 512, 512)

    lane = lax.broadcasted_iota(jnp.int32, (TOK, 128), 1)

    def stat_rows(peak, weight, mean):
        stats = jnp.where(lane == 0, peak, jnp.where(lane == 1, weight, mean))
        return jnp.transpose(stats)[0:8, :]

    out, tangent, *stats = finish(0)
    part_out[:, 0:128] = out.astype(BF16)
    part_out[:, 128:256] = tangent.astype(BF16)
    stat_out[...] = stat_rows(*stats)
    stat_copy = start(remote(stat_out, stat_in, st_sem.at[0], st_sem.at[1], peer(dx=1)))

    def piece(k):
        return pl.ds(pl.multiple_of(lax.rem(z + k, NZ) * PIECE, PIECE), PIECE)

    part_copies = {}
    for k in ORDER:
        rows = piece(k)
        part_copies[k] = start(remote(part_out.at[rows], part_in.at[rows], p_s.at[0], p_r.at[k], peer(dx=1)))
    attend(TOK, TOK, 2, 512, 512)
    out, tangent, *stats = finish(TOK)
    own_part[:, 0:128] = out
    own_part[:, 128:256] = tangent
    own = stat_rows(*stats)
    stat_copy.wait_recv()
    peak, weight, mean = own[0:1, :], own[1:2, :], own[2:3, :]
    peak2, weight2, mean2 = stat_in[0:1, :], stat_in[1:2, :], stat_in[2:3, :]
    high = jnp.maximum(peak, peak2)
    mass = weight * jnp.exp2(peak - high)
    mass2 = weight2 * jnp.exp2(peak2 - high)
    inverse = 1.0 / (mass + mass2)
    p1, p2 = mass * inverse, mass2 * inverse
    p3 = p1 * p2 * (mean - mean2)
    columns = jnp.transpose(jnp.concatenate([p1, p2, p3, jnp.zeros((125, TOK), F32)], axis=0))
    for i in range(3):
        coef[i] = jnp.broadcast_to(columns[:, i : i + 1], (TOK, 128))

    a_copies = {}
    for k in ORDER:
        rows = piece(k)
        if k == 1:
            w_arrived(4)
        part_copies[k].wait_recv()
        o1, u1 = own_part[rows, 0:128], own_part[rows, 128:256]
        o2, u2 = part_in[rows, 0:128].astype(F32), part_in[rows, 128:256].astype(F32)
        c1, c2, c3 = coef[0, rows, :], coef[1, rows, :], coef[2, rows, :]
        merged = (c1 * o1 + c2 * o2).astype(BF16)
        tmerged = (c1 * u1 + c2 * u2 + c3 * (o1 - o2)).astype(BF16)
        if k == 0:
            a_in[0:PIECE, 0:128] = merged
            a_in[PIECE : 2 * PIECE, 0:128] = tmerged
        else:
            a_out[k, 0:PIECE, :] = merged
            a_out[k, PIECE : 2 * PIECE, :] = tmerged
            back = NZ - k
            dst = a_in.at[:, back * 128 : back * 128 + 128]
            a_copies[k] = start(remote(a_out.at[k], dst, a_s.at[0], a_r.at[back], peer(dz=k)))

    for slot in range(1, NZ):
        w_shared(slot)
    for k in range(1, NZ):
        a_copies[k].wait_recv()

    def columns(b, k):
        column = (lax.rem(xh + b, NH) * NZ + lax.rem(z + k, NZ)) * 128
        return w_all[:, :, pl.ds(pl.multiple_of(column, 128), 128)].reshape(NZ * 128, 128)

    g_copies = {}
    for k in ORDER:
        both = dot(a_in[...], jnp.concatenate([columns(1, k), columns(0, k)], axis=1))
        g_out[k] = both[:, 0:128].astype(BF16)
        g_copies[k] = start(remote(g_out.at[k], g_in.at[k], g_s.at[0], g_r.at[k], peer(dh=1)))
        g_own[k] = both[:, 128:256]
    for k in ORDER:
        g_copies[k].wait_recv()
        term = (g_own[k] + g_in[k].astype(F32)).astype(BF16)
        if k == 0:
            out_ref[piece(0), :] = term[0:PIECE]
            tout_ref[piece(0), :] = term[PIECE : 2 * PIECE]
        else:
            f_out[k] = term
            start(remote(f_out.at[k], f_in.at[NZ - k], f_s.at[0], f_r.at[NZ - k], peer(dz=k)))
    sent(kv_s.at[0], xt.at[pl.ds(0, 6 * 64)])
    sent(sib_s.at[0], xt.at[pl.ds(0, 8 * 64)])
    sent(w_s.at[0], xt.at[pl.ds(0, 7 * 64)])
    sent(ws_s.at[0], xt.at[pl.ds(0, 7 * 64)])
    sent(p_s.at[0], part_out)
    sent(a_s.at[0], a_out.at[pl.ds(1, NZ - 1)])
    sent(g_s.at[0], g_out)
    q_copy.wait_send()
    stat_copy.wait_send()
    for k in ORDER:
        if k != 0:
            remote(f_in.at[k], f_in.at[k], f_s.at[0], f_r.at[k], peer(dz=k)).wait_recv()
            out_ref[piece(k), :] = f_in[k, 0:PIECE]
            tout_ref[piece(k), :] = f_in[k, PIECE : 2 * PIECE]
    sent(f_s.at[0], f_out.at[pl.ds(1, NZ - 1)])


def local(inputs, tangents, w_qkv, w_out):
    dma = pltpu.SemaphoreType.DMA
    vmem = pltpu.VMEM
    result = pl.pallas_call(
        kernel,
        name="tangent_attention",
        out_shape=pltpu.VMEM((2 * TOK, 128), BF16),
        in_specs=[pl.BlockSpec(memory_space=pl.ANY)] * 4,
        out_specs=pl.BlockSpec(memory_space=pltpu.VMEM),
        scratch_shapes=[
            vmem((2 * TOK, D), BF16),
            vmem((D, 384), BF16),
            vmem((NY, 1024, 512), BF16),
            vmem((2 * TOK, 256), BF16),
            vmem((2 * TOK, 256), F32),
            vmem((2 * TOK, 128), F32),
            vmem((2 * TOK, 128), F32),
            vmem((2 * TOK, 128), F32),
            vmem((TOK, 256), BF16),
            vmem((TOK, 256), BF16),
            vmem((8, TOK), F32),
            vmem((8, TOK), F32),
            vmem((TOK, 256), F32),
            vmem((3, TOK, 128), F32),
            vmem((NZ, 128, 128), BF16),
            vmem((128, NZ * 128), BF16),
            vmem((NZ, 128, D), BF16),
            vmem((NZ, 128, 128), BF16),
            vmem((NZ, 128, 128), BF16),
            vmem((NZ, 128, 128), F32),
            vmem((NZ, 128, 128), BF16),
            vmem((NZ, 128, 128), BF16),
            dma((8,)),
            dma((1,)),
            dma((NY, 2)),
            dma((1,)),
            dma((NY, 2)),
            dma((2,)),
            dma((1,)),
            dma((8,)),
            dma((1,)),
            dma((8,)),
            dma((1,)),
            dma((8,)),
            dma((2,)),
            dma((1,)),
            dma((8,)),
            dma((1,)),
            dma((8,)),
            dma((1,)),
            dma((8,)),
        ],
        compiler_params=pltpu.CompilerParams(
            collective_id=0, has_side_effects=True, vmem_limit_bytes=58 * 2**20
        ),
    )(inputs, tangents, w_qkv, w_out)
    return result[:TOK], result[TOK:]


def solution(mesh):
    return jax.shard_map(
        local,
        mesh=mesh,
        in_specs=(P("ctx", None), P("ctx", None), P(None, None, "head"), P("head", None)),
        out_specs=(P("ctx", "head"), P("ctx", "head")),
        check_vma=False,
    )
```
